32 devices in a mesh: slab: 8 (over y, x, core), blk: 4 (over z).
Axes of the slice: x: 2, y: 2, z: 4, core: 2. Of those that a mesh axis runs over, the one named last changes fastest.
Arguments:
- queries: bfloat16 [1024, 768], P(('slab', 'blk')), may hold values from -6 to 6
- passages: bfloat16 [1024, 768], P(('blk', 'slab')), may hold values from -6 to 6
- query_lognorm: float32 [1024], P(('slab', 'blk')), as said below
- passage_lognorm: float32 [1024], P('blk'), as said below
- loss_cotangent: float32 [], replicated, may hold values from 4 to 12
Outputs:
- query_gradient: float32 [1024, 768], P(('slab', 'blk'))
- passage_gradient: float32 [1024, 768], P(('blk', 'slab'))
The draws below stay inside these ranges and needn't reach their ends.
Inputs may be any that keep to these rules, and one draw needn't show every extreme that they name: `query_lognorm`: every entry lies between log(1024) + 0.5 and log(1024) + 3.5. `passage_lognorm`: every entry lies between log(1024) + 0.5 and log(1024) + 3.5.
All inputs are finite; a program needn't handle non-finite values.
Results may differ from the reference program's by a relative error of at most 0.034.
Values may be sent and summed in bfloat16 or wider, within the bound.
No kernel may reach another device: no remote copies, remote signals or barrier semaphores. Data moves between devices by JAX's collectives and lax.ppermute only.
A program may use at most 64 MiB of HBM per device.

```python
import math
import jax
import jax.numpy as jnp
from jax import lax

D = 768
BATCH = 1024
N_SLAB = 8


def lognorm_values(key):
    offset = jnp.log(jnp.float32(BATCH))
    unit_draw = jax.random.uniform(key, (BATCH,), jnp.float32)
    return offset + 0.5 + 3.0 * unit_draw


def draw_query_lognorm(key, part):
    return lognorm_values(jax.random.fold_in(key, 11))


def draw_passage_lognorm(key, part):
    return lognorm_values(jax.random.fold_in(key, 23))


def shard_levels(rng, dims, split, smallest, top_value):
    def one(dim, blocks):
        draws = jax.random.uniform(jax.random.fold_in(jax.random.fold_in(rng, 6), dim), (blocks,), jnp.float32, smallest / len(split), top_value / len(split))
        return jnp.repeat(jnp.exp(draws), dims[dim] // blocks).reshape((-1,) + (1,) * (len(dims) - dim - 1))

    factor_of = one(*split[0])
    for cut in split[1:]:
        factor_of = factor_of * one(*cut)
    return factor_of


def scatter_about(stream_key, shape, scale, limit, cuts=(), kind=jnp.bfloat16):
    values = scale * jax.random.normal(stream_key, shape, jnp.float32)
    if cuts:
        values = values * shard_levels(stream_key, shape, cuts, -0.22, 0.18)
    return jnp.clip(values, -limit, limit).astype(kind)


def setup_inputs(seed: int = 0) -> dict:
    streams_of = jax.random.split(jax.random.key(seed), 6)
    queries = scatter_about(streams_of[0], (BATCH, D), 1.0, 6.0, ((0, 32),))
    passages = scatter_about(streams_of[1], (BATCH, D), 1.0, 6.0, ((0, 32),))
    query_lognorm = draw_query_lognorm(jax.random.fold_in(streams_of[5], 71), 0)
    passage_lognorm = draw_passage_lognorm(jax.random.fold_in(streams_of[5], 71), 0)
    loss_cotangent = jnp.clip(jax.random.uniform(streams_of[4], (), jnp.float32, 4.0, 12.0), 4.0, 12.0)
    return dict(queries=queries, passages=passages, query_lognorm=query_lognorm, passage_lognorm=passage_lognorm, loss_cotangent=loss_cotangent)


def reference(queries, passages, query_lognorm, passage_lognorm, loss_cotangent):
    score_scale = 2.0 / math.sqrt(D)
    half_cotangent = 0.5 * loss_cotangent
    query_blocks = queries.reshape(N_SLAB, BATCH // N_SLAB, D)
    norm_blocks = query_lognorm.reshape(N_SLAB, BATCH // N_SLAB)
    column_numbers = jnp.arange(BATCH, dtype=jnp.int32)
    block_numbers = jnp.arange(N_SLAB, dtype=jnp.int32)
    passages_wide = passages.astype(jnp.float32)

    def block_step(passage_total, inputs):
        query_rows, query_norms, block_index = inputs
        block_rows = query_rows.shape[0]
        scores = score_scale * lax.dot_general(query_rows, passages, (((1,), (1,)), ((), ())), preferred_element_type=jnp.float32)
        row_numbers = block_index * block_rows + jnp.arange(block_rows, dtype=jnp.int32)
        paired = (row_numbers[:, None] == column_numbers[None, :]).astype(jnp.float32)
        weights = half_cotangent * (jnp.exp(scores - query_norms[:, None]) + jnp.exp(scores - passage_lognorm[None, :]) - 2.0 * paired)
        rows_wide = query_rows.astype(jnp.float32)
        query_term = score_scale * jnp.dot(weights, passages_wide, precision=lax.Precision.HIGHEST, preferred_element_type=jnp.float32)
        passage_term = score_scale * lax.dot_general(weights, rows_wide, (((0,), (0,)), ((), ())), precision=lax.Precision.HIGHEST, preferred_element_type=jnp.float32)
        return (passage_total + passage_term, query_term)
    passage_total, query_terms = lax.scan(block_step, jnp.zeros((BATCH, D), jnp.float32), (query_blocks, norm_blocks, block_numbers))
    return (query_terms.reshape(BATCH, D), passage_total)
```

```python
import functools
import math

import jax
import jax.numpy as jnp
from jax import lax
from jax.experimental import pallas as pl
from jax.experimental.pallas import tpu as pltpu
from jax.sharding import PartitionSpec as P

AXES = ("slab", "blk")
TAIL = 128


def split_three(values):
    high = values.astype(jnp.bfloat16)
    rest = values - high.astype(jnp.float32)
    middle = rest.astype(jnp.bfloat16)
    low = (rest - middle.astype(jnp.float32)).astype(jnp.bfloat16)
    return high, middle, low


def peer(index, step, count):
    if count & (count - 1) == 0:
        return index ^ step
    return (index + step) % count


class Plan:
    def __init__(self, slab_count, blk_count):
        self.blk_count = blk_count
        self.chip_count = slab_count // 2
        self.group_size = max(self.chip_count, blk_count)

    def device(self, chip, core, blk):
        return (2 * chip + core) * self.blk_count + blk

    def each(self):
        for chip in range(self.chip_count):
            for blk in range(self.blk_count):
                yield chip, blk

    def core_pairs(self):
        return [
            (self.device(chip, core, blk), self.device(chip, 1 - core, blk))
            for chip, blk in self.each()
            for core in (0, 1)
        ]

    def one_way(self, core):
        return [
            (self.device(chip, core, blk), self.device(chip, 1 - core, blk))
            for chip, blk in self.each()
        ]

    def group_pairs(self, step):
        pairs = []
        for chip, blk in self.each():
            if step < self.chip_count:
                other = peer(chip, step, self.chip_count)
                pairs.append((self.device(chip, 0, blk), self.device(other, 0, blk)))
            if step < self.blk_count:
                other = peer(blk, step, self.blk_count)
                pairs.append((self.device(chip, 1, blk), self.device(chip, 1, other)))
        return pairs


def pack_kernel(core_ref, q_ref, p_ref, got_q_ref, got_p_ref, norms_ref, out_ref):
    rows, width = q_ref.shape
    is_query = core_ref[0] == 1
    out_ref[:rows, :width] = jnp.where(is_query, q_ref[...], p_ref[...])
    out_ref[rows:, :width] = jnp.where(is_query, got_q_ref[...], got_p_ref[...])
    high, middle, low = split_three(norms_ref[...])
    lane = lax.broadcasted_iota(jnp.int32, (2 * rows, TAIL), 1)
    spread = functools.partial(jnp.broadcast_to, shape=(2 * rows, TAIL))
    out_ref[:, width:] = jnp.where(
        lane == 0,
        spread(high.astype(jnp.float32)),
        jnp.where(
            lane == 1,
            spread(middle.astype(jnp.float32)),
            jnp.where(lane == 2, spread(low.astype(jnp.float32)), 0.0),
        ),
    ).astype(jnp.bfloat16)


def tile_kernel(count, half_ref, row_ref, column_ref, *refs):
    a_refs, b_refs, out_refs = refs[:count], refs[count : 2 * count], refs[2 * count :]
    rows, wide = a_refs[0].shape
    width = wide - TAIL
    scale = 2.0 / math.sqrt(width)
    a = jnp.concatenate([r[...] for r in a_refs], axis=0)
    b = jnp.concatenate([r[...] for r in b_refs], axis=0)
    contract = (((1,), (1,)), ((), ()))
    scores = scale * lax.dot_general(
        a[:, :width], b[:, :width], contract, preferred_element_type=jnp.float32
    )
    tail = a[:, width:].astype(jnp.float32)
    a_norm = tail[:, 0:1] + tail[:, 1:2] + tail[:, 2:3]
    ones = jnp.ones((16, TAIL), jnp.bfloat16)
    b_norm = lax.dot_general(ones, b[:, width:], contract, preferred_element_type=jnp.float32)[0:1]
    paired = (row_ref[...] == column_ref[...]).astype(jnp.float32)
    weights = half_ref[0] * (
        jnp.exp(scores - a_norm) + jnp.exp(scores - b_norm) - 2.0 * paired
    )
    high = weights.astype(jnp.bfloat16)
    low = (weights - high.astype(jnp.float32)).astype(jnp.bfloat16)
    total = jnp.dot(high, b[:, :width], preferred_element_type=jnp.float32) + jnp.dot(
        low, b[:, :width], preferred_element_type=jnp.float32
    )
    total = scale * total
    for i, out_ref in enumerate(out_refs):
        out_ref[...] = total[i * rows : (i + 1) * rows]


VMEM = pl.BlockSpec(memory_space=pltpu.VMEM)
SMEM = pl.BlockSpec(memory_space=pltpu.SMEM)


def local(plan, queries, passages, query_lognorm, passage_lognorm, loss_cotangent):
    rows, width = queries.shape
    wide = width + TAIL
    count = plan.group_size
    slab = lax.axis_index("slab")
    blk = lax.axis_index("blk")
    chip, core = slab // 2, slab % 2

    got_q = lax.ppermute(queries, AXES, plan.one_way(0))
    got_p = lax.ppermute(passages, AXES, plan.one_way(1))
    got_norm = lax.ppermute(query_lognorm, AXES, plan.one_way(0))
    p_norms = passage_lognorm.reshape(-1, rows)
    own_first = jnp.stack([p_norms[slab], p_norms[slab ^ 1]]).reshape(-1)
    norms = jnp.where(core == 1, jnp.concatenate([query_lognorm, got_norm]), own_first)
    mine = pl.pallas_call(
        pack_kernel,
        out_shape=jax.ShapeDtypeStruct((2 * rows, wide), jnp.bfloat16),
        in_specs=[SMEM] + [VMEM] * 5,
        out_specs=VMEM,
        name="pack",
    )(core.reshape(1), queries, passages, got_q, got_p, norms[:, None])

    a_parts, b_parts = [mine], []
    for step in range(1, count):
        back = [(to, at) for at, to in plan.group_pairs(step)]
        a_parts.append(lax.ppermute(mine, AXES, back))
    b_parts = [lax.ppermute(part, AXES, plan.core_pairs()) for part in a_parts]

    def numbers(role):
        at = lax.broadcasted_iota(jnp.int32, (count, 2, rows), 0)
        of = lax.broadcasted_iota(jnp.int32, (count, 2, rows), 1) ^ role
        within = lax.broadcasted_iota(jnp.int32, (count, 2, rows), 2)
        p_shard = blk * (2 * plan.chip_count) + 2 * peer(chip, at, plan.chip_count) + of
        q_shard = (2 * chip + of) * plan.blk_count + peer(blk, at, plan.blk_count)
        p_number = jnp.where(at < plan.chip_count, p_shard * rows + within, -1)
        q_number = jnp.where(at < plan.blk_count, q_shard * rows + within, -2)
        return jnp.where(role == 0, p_number, q_number).reshape(-1)

    partials = pl.pallas_call(
        functools.partial(tile_kernel, count),
        out_shape=[jax.ShapeDtypeStruct((2 * rows, width), jnp.float32)] * count,
        in_specs=[SMEM] + [VMEM] * (2 * count + 2),
        out_specs=[VMEM] * count,
        name="tile",
        compiler_params=pltpu.CompilerParams(vmem_limit_bytes=48 * 1024 * 1024),
    )(
        (0.5 * loss_cotangent).reshape(1),
        numbers(core)[:, None],
        numbers(1 - core)[None, :],
        *a_parts,
        *b_parts,
    )

    total = partials[0]
    for step in range(1, count):
        total = total + lax.ppermute(partials[step], AXES, plan.group_pairs(step))
    own = total[:rows]
    got = lax.ppermute(total[rows:], AXES, plan.core_pairs())
    return jnp.where(core == 1, own, got), jnp.where(core == 1, got, own)


def solution(mesh):
    plan = Plan(mesh.shape["slab"], mesh.shape["blk"])
    return jax.shard_map(
        functools.partial(local, plan),
        mesh=mesh,
        in_specs=(
            P(("slab", "blk"), None),
            P(("blk", "slab"), None),
            P(("slab", "blk")),
            P("blk"),
            P(),
        ),
        out_specs=(P(("slab", "blk"), None), P(("blk", "slab"), None)),
        check_vma=False,
    )
```

```python
import functools
import math

import jax
import jax.numpy as jnp
from jax import lax
from jax.experimental import pallas as pl
from jax.experimental.pallas import tpu as pltpu
from jax.sharding import PartitionSpec as P

AXES = ("slab", "blk")
TAIL = 128


def split_three(values):
    high = values.astype(jnp.bfloat16)
    rest = values - high.astype(jnp.float32)
    middle = rest.astype(jnp.bfloat16)
    low = (rest - middle.astype(jnp.float32)).astype(jnp.bfloat16)
    return high, middle, low


def peer(index, step, count):
    if count & (count - 1) == 0:
        return index ^ step
    return (index + step) % count


class Plan:
    def __init__(self, slab_count, blk_count):
        self.blk_count = blk_count
        self.chip_count = slab_count // 2
        self.group_size = max(self.chip_count, blk_count)

    def device(self, chip, core, blk):
        return (2 * chip + core) * self.blk_count + blk

    def each(self):
        for chip in range(self.chip_count):
            for blk in range(self.blk_count):
                yield chip, blk

    def core_pairs(self):
        return [
            (self.device(chip, core, blk), self.device(chip, 1 - core, blk))
            for chip, blk in self.each()
            for core in (0, 1)
        ]

    def group_pairs(self, step):
        pairs = []
        for chip, blk in self.each():
            if step < self.chip_count:
                other = peer(chip, step, self.chip_count)
                pairs.append((self.device(chip, 0, blk), self.device(other, 0, blk)))
            if step < self.blk_count:
                other = peer(blk, step, self.blk_count)
                pairs.append((self.device(chip, 1, blk), self.device(chip, 1, other)))
        return pairs


def column(values, first, rows):
    shape = (rows, values.shape[1])
    lane = lax.broadcasted_iota(jnp.int32, shape, 1)
    row = lax.broadcasted_iota(jnp.int32, shape, 0)
    picked = jnp.where(lane == row + first, jnp.broadcast_to(values, shape), 0.0)
    return jnp.sum(picked, axis=1, keepdims=True)


def with_tail(out_ref, start, block, norms):
    rows, width = block.shape
    high, middle, low = (
        jnp.broadcast_to(part.astype(jnp.float32), (rows, TAIL)) for part in split_three(norms)
    )
    lane = lax.broadcasted_iota(jnp.int32, (rows, TAIL), 1)
    tail = jnp.where(lane == 0, high, jnp.where(lane == 1, middle, low))
    out_ref[start : start + rows, :width] = block
    out_ref[start : start + rows, width:] = jnp.where(lane < 3, tail, 0.0).astype(jnp.bfloat16)


def pack_kernel(
    slab_ref, q_ref, p_ref, got_q_ref, got_p_ref, norm_ref, got_norm_ref, p_norm_ref, a_ref, b_ref
):
    rows = q_ref.shape[0]
    slab = slab_ref[0]
    is_query = (slab & 1) == 1
    own_q = column(norm_ref[...], 0, rows)
    got_q = column(got_norm_ref[...], 0, rows)
    own_p = column(p_norm_ref[...], slab * rows, rows)
    got_p = column(p_norm_ref[...], (slab ^ 1) * rows, rows)
    pick = functools.partial(jnp.where, is_query)
    with_tail(a_ref, 0, pick(q_ref[...], p_ref[...]), pick(own_q, own_p))
    with_tail(a_ref, rows, pick(got_q_ref[...], got_p_ref[...]), pick(got_q, got_p))
    with_tail(b_ref, 0, pick(got_p_ref[...], got_q_ref[...]), pick(got_p, got_q))
    with_tail(b_ref, rows, pick(p_ref[...], q_ref[...]), pick(own_p, own_q))


def row_numbers(plan, slab, blk, role, rows, place):
    chip = slab >> 1
    number = place
    for step in range(plan.group_size):
        for other in (0, 1):
            core = role ^ other
            p_shard = blk * (2 * plan.chip_count) + 2 * peer(chip, step, plan.chip_count) + core
            q_shard = (2 * chip + core) * plan.blk_count + peer(blk, step, plan.blk_count)
            p_base = p_shard * rows if step < plan.chip_count else -(1 << 24)
            q_base = q_shard * rows if step < plan.blk_count else -(1 << 25)
            start = (2 * step + other) * rows
            base = jnp.where(role == 0, p_base, q_base) - start
            number = jnp.where(place >= start, place + base, number)
    return number


def tile_kernel(plan, slab_ref, blk_ref, loss_ref, *refs):
    count = plan.group_size
    a_refs, b_refs, out_refs = refs[:count], refs[count : 2 * count], refs[2 * count :]
    rows, wide = a_refs[0].shape
    width = wide - TAIL
    scale = 2.0 / math.sqrt(width)
    a = jnp.concatenate([r[...] for r in a_refs], axis=0)
    b = jnp.concatenate([r[...] for r in b_refs], axis=0)
    contract = (((1,), (1,)), ((), ()))
    scores = scale * lax.dot_general(
        a[:, :width], b[:, :width], contract, preferred_element_type=jnp.float32
    )
    tail = a[:, width:].astype(jnp.float32)
    a_norm = tail[:, 0:1] + tail[:, 1:2] + tail[:, 2:3]
    ones = jnp.ones((16, TAIL), jnp.bfloat16)
    b_norm = lax.dot_general(ones, b[:, width:], contract, preferred_element_type=jnp.float32)[0:1]
    slab, blk = slab_ref[0], blk_ref[0]
    role = slab & 1
    numbers = functools.partial(row_numbers, plan, slab, blk, rows=rows // 2)
    a_number = numbers(role, place=lax.broadcasted_iota(jnp.int32, (count * rows, 1), 0))
    b_number = numbers(1 - role, place=lax.broadcasted_iota(jnp.int32, (1, count * rows), 1))
    paired = (a_number == b_number).astype(jnp.float32)
    weights = (0.5 * loss_ref[0]) * (
        jnp.exp(scores - a_norm) + jnp.exp(scores - b_norm) - 2.0 * paired
    )
    high = weights.astype(jnp.bfloat16)
    low = (weights - high.astype(jnp.float32)).astype(jnp.bfloat16)
    total = jnp.dot(high, b[:, :width], preferred_element_type=jnp.float32) + jnp.dot(
        low, b[:, :width], preferred_element_type=jnp.float32
    )
    total = scale * total
    for i, out_ref in enumerate(out_refs):
        out_ref[...] = total[i * rows : (i + 1) * rows]


VMEM = pl.BlockSpec(memory_space=pltpu.VMEM)
SMEM = pl.BlockSpec(memory_space=pltpu.SMEM)


def local(plan, queries, passages, query_lognorm, passage_lognorm, loss_cotangent):
    rows, width = queries.shape
    wide = width + TAIL
    count = plan.group_size
    slab = lax.axis_index("slab")
    blk = lax.axis_index("blk")
    core = slab & 1

    def swapped(block):
        return lax.ppermute(block, AXES, plan.core_pairs())

    packed = jax.ShapeDtypeStruct((2 * rows, wide), jnp.bfloat16)
    mine, others = pl.pallas_call(
        pack_kernel,
        out_shape=[packed, packed],
        in_specs=[SMEM] + [VMEM] * 7,
        out_specs=[VMEM, VMEM],
        name="pack",
        compiler_params=pltpu.CompilerParams(vmem_limit_bytes=4 * 1024 * 1024),
    )(
        slab.reshape(1),
        queries,
        passages,
        swapped(queries),
        swapped(passages),
        query_lognorm.reshape(1, -1),
        swapped(query_lognorm).reshape(1, -1),
        passage_lognorm.reshape(1, -1),
    )

    a_parts, b_parts = [mine], [others]
    for step in range(1, count):
        back = [(to, at) for at, to in plan.group_pairs(step)]
        a_parts.append(lax.ppermute(mine, AXES, back))
        b_parts.append(swapped(a_parts[-1]))

    partials = pl.pallas_call(
        functools.partial(tile_kernel, plan),
        out_shape=[jax.ShapeDtypeStruct((2 * rows, width), jnp.float32)] * count,
        in_specs=[SMEM] * 3 + [VMEM] * (2 * count),
        out_specs=[VMEM] * count,
        name="tile",
        compiler_params=pltpu.CompilerParams(vmem_limit_bytes=3 * count * 1024 * 1024),
    )(slab.reshape(1), blk.reshape(1), loss_cotangent.reshape(1), *a_parts, *b_parts)

    total = partials[0]
    for step in range(1, count):
        total = total + lax.ppermute(partials[step], AXES, plan.group_pairs(step))
    own = total[:rows]
    got = swapped(total[rows:])
    return jnp.where(core == 1, own, got), jnp.where(core == 1, got, own)


def solution(mesh):
    plan = Plan(mesh.shape["slab"], mesh.shape["blk"])
    return jax.shard_map(
        functools.partial(local, plan),
        mesh=mesh,
        in_specs=(
            P(("slab", "blk"), None),
            P(("blk", "slab"), None),
            P(("slab", "blk")),
            P("blk"),
            P(),
        ),
        out_specs=(P(("slab", "blk"), None), P(("blk", "slab"), None)),
        check_vma=False,
    )
```

```python
import functools
import math

import jax
import jax.numpy as jnp
from jax import lax
from jax.experimental import pallas as pl
from jax.experimental.pallas import tpu as pltpu
from jax.sharding import PartitionSpec as P

AXES = ("slab", "blk")
LANES = 128
NORM_ROWS = 16
SIZE_ROWS = 8
ORDER = ((3, 2, 1), (3, 2, 1))
BACK_ORDER = ((1, 2, 3), (1, 2, 3))


def peer(index, step, count):
    if count & (count - 1) == 0:
        return index ^ step
    return (index + step) % count


class Plan:
    def __init__(self, slab_count, blk_count):
        self.blk_count = blk_count
        self.chip_count = slab_count // 2
        self.group_size = max(self.chip_count, blk_count)

    def device(self, chip, core, blk):
        return (2 * chip + core) * self.blk_count + blk

    def each(self):
        for chip in range(self.chip_count):
            for blk in range(self.blk_count):
                yield chip, blk

    def core_pairs(self):
        return [
            (self.device(chip, core, blk), self.device(chip, 1 - core, blk))
            for chip, blk in self.each()
            for core in (0, 1)
        ]

    def group_pairs(self, step):
        pairs = []
        for chip, blk in self.each():
            if step < self.chip_count:
                other = peer(chip, step, self.chip_count)
                pairs.append((self.device(chip, 0, blk), self.device(other, 0, blk)))
            if step < self.blk_count:
                other = peer(blk, step, self.blk_count)
                pairs.append((self.device(chip, 1, blk), self.device(chip, 1, other)))
        return pairs


def column(values, first, rows):
    shape = (rows, values.shape[1])
    lane = lax.broadcasted_iota(jnp.int32, shape, 1)
    row = lax.broadcasted_iota(jnp.int32, shape, 0)
    picked = jnp.where(lane == row + first, jnp.broadcast_to(values, shape), 0.0)
    return jnp.sum(picked, axis=1, keepdims=True)


def as_row(values, lanes):
    shape = (values.shape[0], lanes)
    lane = lax.broadcasted_iota(jnp.int32, shape, 1)
    row = lax.broadcasted_iota(jnp.int32, shape, 0)
    picked = jnp.where(lane == row, jnp.broadcast_to(values, shape), 0.0)
    return jnp.sum(picked, axis=0, keepdims=True)


def split_three(values):
    high = values.astype(jnp.bfloat16).astype(jnp.float32)
    middle = (values - high).astype(jnp.bfloat16).astype(jnp.float32)
    return high, middle, values - high - middle


def write_block(out_ref, halves, norms):
    rows, width = halves[0].shape
    for chunk in range(width // LANES):
        for half in (0, 1):
            start = (2 * chunk + half) * rows
            out_ref[start : start + rows] = halves[half][:, chunk * LANES : (chunk + 1) * LANES]
    shape = (NORM_ROWS, LANES)
    row = lax.broadcasted_iota(jnp.int32, shape, 0)
    tail = jnp.zeros(shape, jnp.float32)
    for half in (0, 1):
        for i, part in enumerate(split_three(as_row(norms[half], LANES))):
            tail = jnp.where(row == 3 * half + i, jnp.broadcast_to(part, shape), tail)
    out_ref[2 * rows * (width // LANES) :] = tail.astype(jnp.bfloat16)


def read_block(ref, rows):
    chunks = (ref.shape[0] - NORM_ROWS) // (2 * rows)
    block = jnp.concatenate(
        [ref[2 * rows * i : 2 * rows * (i + 1)] for i in range(chunks)], axis=1
    )
    tail = ref[2 * rows * chunks :].astype(jnp.float32)
    norms = [
        column(tail[i : i + 1] + tail[i + 1 : i + 2] + tail[i + 2 : i + 3], 0, rows) for i in (0, 3)
    ]
    return block, jnp.concatenate(norms, axis=0)


def pack_kernel(
    slab_ref, role_ref, other_ref, got_q_ref, got_p_ref, norm_ref, got_norm_ref, a_ref, b_ref
):
    rows = role_ref.shape[0]
    slab = slab_ref[0]
    pick = functools.partial(jnp.where, (slab & 1) == 1)
    own_q = column(norm_ref[...], 0, rows)
    got_q = column(got_norm_ref[...], 0, rows)
    own_p = column(norm_ref[...], (1 + slab) * rows, rows)
    got_p = column(norm_ref[...], (1 + (slab ^ 1)) * rows, rows)
    write_block(
        a_ref,
        (role_ref[...], pick(got_q_ref[...], got_p_ref[...])),
        (pick(own_q, own_p), pick(got_q, got_p)),
    )
    write_block(
        b_ref,
        (pick(got_p_ref[...], got_q_ref[...]), other_ref[...]),
        (pick(got_p, got_q), pick(own_p, own_q)),
    )


def row_numbers(plan, slab, blk, role, rows, place):
    chip = slab >> 1
    number = place
    for step in range(plan.group_size):
        for other in (0, 1):
            core = role ^ other
            p_shard = blk * (2 * plan.chip_count) + 2 * peer(chip, step, plan.chip_count) + core
            q_shard = (2 * chip + core) * plan.blk_count + peer(blk, step, plan.blk_count)
            p_base = p_shard * rows if step < plan.chip_count else -(1 << 24)
            q_base = q_shard * rows if step < plan.blk_count else -(1 << 25)
            start = (2 * step + other) * rows
            base = jnp.where(role == 0, p_base, q_base) - start
            number = jnp.where(place >= start, place + base, number)
    return number


def tile_kernel(plan, rows, slab_ref, blk_ref, loss_ref, *refs):
    count = plan.group_size
    a_refs, b_refs, out_refs = refs[:count], refs[count : 2 * count], refs[2 * count :]
    a, a_norm = (jnp.concatenate(x, axis=0) for x in zip(*(read_block(r, rows) for r in a_refs)))
    b, b_norm = (jnp.concatenate(x, axis=0) for x in zip(*(read_block(r, rows) for r in b_refs)))
    b_norm = as_row(b_norm, b_norm.shape[0])
    scale = 2.0 / math.sqrt(a.shape[1])
    scores = scale * lax.dot_general(
        a, b, (((1,), (1,)), ((), ())), preferred_element_type=jnp.float32
    )
    slab, blk = slab_ref[0], blk_ref[0]
    role = slab & 1
    numbers = functools.partial(row_numbers, plan, slab, blk, rows=rows)
    a_number = numbers(role, place=lax.broadcasted_iota(jnp.int32, (a.shape[0], 1), 0))
    b_number = numbers(1 - role, place=lax.broadcasted_iota(jnp.int32, (1, b.shape[0]), 1))
    paired = (a_number == b_number).astype(jnp.float32)
    weights = (0.5 * loss_ref[0]) * (
        jnp.exp(scores - a_norm) + jnp.exp(scores - b_norm) - 2.0 * paired
    )
    high = weights.astype(jnp.bfloat16)
    low = (weights - high.astype(jnp.float32)).astype(jnp.bfloat16)
    total = jnp.dot(high, b, preferred_element_type=jnp.float32) + jnp.dot(
        low, b, preferred_element_type=jnp.float32
    )
    total = scale * total
    out_refs[0][...] = total[: 2 * rows]
    for i in range(1, count):
        write_partial(out_refs[i], total[2 * rows * i : 2 * rows * (i + 1)])


def write_partial(ref, block):
    rows, width = block.shape
    largest = jnp.maximum(jnp.max(jnp.abs(block), keepdims=True), 1e-30)
    power = jnp.ceil(jnp.log2(largest)) - 10.0
    block = block * jnp.exp2(-power)
    for chunk in range(width // LANES):
        ref[chunk * rows : (chunk + 1) * rows] = block[:, chunk * LANES : (chunk + 1) * LANES]
    ref[rows * (width // LANES) :] = jnp.broadcast_to(power, (SIZE_ROWS, LANES))


def sum_kernel(own_ref, *refs):
    partial_refs, (keep_ref, give_ref) = refs[:-2], refs[-2:]
    rows, width = own_ref.shape
    tail = rows * (width // LANES)
    factors = [jnp.exp2(ref[tail : tail + 1]) for ref in partial_refs]
    for chunk in range(width // LANES):
        lanes = slice(chunk * LANES, (chunk + 1) * LANES)
        total = own_ref[:, lanes]
        for ref, factor in zip(partial_refs, factors):
            total = total + ref[chunk * rows : (chunk + 1) * rows] * factor
        keep_ref[:, lanes] = total[: rows // 2]
        give_ref[:, lanes] = total[rows // 2 :]


VMEM = pl.BlockSpec(memory_space=pltpu.VMEM)
SMEM = pl.BlockSpec(memory_space=pltpu.SMEM)


def call(kernel, name, scalars, arrays, out_shape, mebibytes):
    return pl.pallas_call(
        kernel,
        out_shape=out_shape,
        in_specs=[SMEM] * len(scalars) + [VMEM] * len(arrays),
        out_specs=[VMEM] * len(out_shape),
        name=name,
        compiler_params=pltpu.CompilerParams(vmem_limit_bytes=mebibytes * 1024 * 1024),
    )(*(x.reshape(1) for x in scalars), *arrays)


def local(plan, queries, passages, query_lognorm, passage_lognorm, loss_cotangent):
    rows, width = queries.shape
    count = plan.group_size
    chunk_rows = 2 * rows * (width // LANES)
    slab = lax.axis_index("slab")
    blk = lax.axis_index("blk")
    core = slab & 1

    def swapped(block):
        return lax.ppermute(block, AXES, plan.core_pairs())

    packed = jax.ShapeDtypeStruct((chunk_rows + NORM_ROWS, LANES), jnp.bfloat16)
    mine, others = call(
        pack_kernel,
        "pack",
        (slab,),
        (
            jnp.where(core == 1, queries, passages),
            jnp.where(core == 1, passages, queries),
            swapped(queries),
            swapped(passages),
            jnp.concatenate([query_lognorm, passage_lognorm]).reshape(1, -1),
            swapped(query_lognorm).reshape(1, -1),
        ),
        [packed, packed],
        4,
    )

    a_parts, b_parts = [mine], [others]
    for step in range(1, count):
        back = [(to, at) for at, to in plan.group_pairs(step)]
        a_parts.append(lax.ppermute(mine, AXES, back))
        b_parts.append(swapped(a_parts[-1]))

    whole = jax.ShapeDtypeStruct((2 * rows, width), jnp.float32)
    half = jax.ShapeDtypeStruct((rows, width), jnp.float32)
    partial = jax.ShapeDtypeStruct((chunk_rows + SIZE_ROWS, LANES), jnp.float32)
    own, *partials = call(
        functools.partial(tile_kernel, plan, rows),
        "tile",
        (slab, blk, loss_cotangent),
        (*a_parts, *b_parts),
        [whole] + [partial] * (count - 1),
        3 * count,
    )

    arrived = [
        lax.ppermute(x.astype(jnp.float16), AXES, plan.group_pairs(1 + i)).astype(jnp.float32)
        for i, x in enumerate(partials)
    ]
    keep, give = call(sum_kernel, "sum", (), (own, *arrived), [half, half], 2 * count)
    got = swapped(give)
    return jnp.where(core == 1, keep, got), jnp.where(core == 1, got, keep)


def solution(mesh):
    plan = Plan(mesh.shape["slab"], mesh.shape["blk"])
    return jax.shard_map(
        functools.partial(local, plan),
        mesh=mesh,
        in_specs=(
            P(("slab", "blk"), None),
            P(("blk", "slab"), None),
            P(("slab", "blk")),
            P("blk"),
            P(),
        ),
        out_specs=(P(("slab", "blk"), None), P(("blk", "slab"), None)),
        check_vma=False,
    )
```

```python
import functools
import math

import jax
import jax.numpy as jnp
from jax import lax
from jax.experimental import pallas as pl
from jax.experimental.pallas import tpu as pltpu
from jax.sharding import PartitionSpec as P

AXES = ("slab", "blk")
LANES = 128
NORM_ROWS = 16
SIZE_ROWS = 8


def peer(index, step, count):
    if count & (count - 1) == 0:
        return index ^ step
    return (index + step) % count


class Plan:
    def __init__(self, slab_count, blk_count):
        self.blk_count = blk_count
        self.chip_count = slab_count // 2
        self.group_size = max(self.chip_count, blk_count)

    def device(self, chip, core, blk):
        return (2 * chip + core) * self.blk_count + blk

    def each(self):
        for chip in range(self.chip_count):
            for blk in range(self.blk_count):
                yield chip, blk

    def core_pairs(self):
        return [
            (self.device(chip, core, blk), self.device(chip, 1 - core, blk))
            for chip, blk in self.each()
            for core in (0, 1)
        ]

    def group_pairs(self, step):
        pairs = []
        for chip, blk in self.each():
            if step < self.chip_count:
                other = peer(chip, step, self.chip_count)
                pairs.append((self.device(chip, 0, blk), self.device(other, 0, blk)))
            if step < self.blk_count:
                other = peer(blk, step, self.blk_count)
                pairs.append((self.device(chip, 1, blk), self.device(chip, 1, other)))
        return pairs


def column(values, first, rows):
    shape = (rows, values.shape[1])
    lane = lax.broadcasted_iota(jnp.int32, shape, 1)
    row = lax.broadcasted_iota(jnp.int32, shape, 0)
    picked = jnp.where(lane == row + first, jnp.broadcast_to(values, shape), 0.0)
    return jnp.sum(picked, axis=1, keepdims=True)


def as_row(values, lanes):
    shape = (values.shape[0], lanes)
    lane = lax.broadcasted_iota(jnp.int32, shape, 1)
    row = lax.broadcasted_iota(jnp.int32, shape, 0)
    picked = jnp.where(lane == row, jnp.broadcast_to(values, shape), 0.0)
    return jnp.sum(picked, axis=0, keepdims=True)


def split_three(values):
    high = values.astype(jnp.bfloat16).astype(jnp.float32)
    middle = (values - high).astype(jnp.bfloat16).astype(jnp.float32)
    return high, middle, values - high - middle


def write_block(out_ref, halves, norms):
    rows, width = halves[0].shape
    for chunk in range(width // LANES):
        for half in (0, 1):
            start = (2 * chunk + half) * rows
            out_ref[start : start + rows] = halves[half][:, chunk * LANES : (chunk + 1) * LANES]
    shape = (NORM_ROWS, LANES)
    row = lax.broadcasted_iota(jnp.int32, shape, 0)
    tail = jnp.zeros(shape, jnp.float32)
    for half in (0, 1):
        for i, part in enumerate(split_three(as_row(norms[half], LANES))):
            tail = jnp.where(row == 3 * half + i, jnp.broadcast_to(part, shape), tail)
    out_ref[2 * rows * (width // LANES) :] = tail.astype(jnp.bfloat16)


def read_rows(refs, rows):
    size = 2 * rows
    chunks = (refs[0].shape[0] - NORM_ROWS) // size
    parts = [[ref[size * i : size * (i + 1)] for i in range(chunks)] for ref in refs]
    return jnp.concatenate([jnp.concatenate(part, axis=1) for part in parts], axis=0)


def read_norms(refs):
    norms = []
    for ref in refs:
        tail = ref[ref.shape[0] - NORM_ROWS :].astype(jnp.float32)
        norms += [tail[i : i + 1] + tail[i + 1 : i + 2] + tail[i + 2 : i + 3] for i in (0, 3)]
    return norms


def norm_column(refs, rows):
    return jnp.concatenate([column(norm, 0, rows) for norm in read_norms(refs)], axis=0)


def norm_row(refs, rows):
    norms, per_row = read_norms(refs), LANES // rows
    lane = lax.broadcasted_iota(jnp.int32, (1, LANES), 1)
    pieces = []
    for start in range(0, len(norms), per_row):
        piece = norms[start]
        for i, norm in enumerate(norms[start + 1 : start + per_row], 1):
            piece = jnp.where(lane >= i * rows, pltpu.roll(norm, i * rows, 1), piece)
        pieces.append(piece)
    return jnp.concatenate(pieces, axis=1)[:, : len(norms) * rows]


def pack_kernel(
    slab_ref, role_ref, other_ref, got_q_ref, got_p_ref, norm_ref, got_norm_ref, a_ref, b_ref
):
    rows = role_ref.shape[0]
    slab = slab_ref[0]
    pick = functools.partial(jnp.where, (slab & 1) == 1)
    own_q = column(norm_ref[...], 0, rows)
    got_q = column(got_norm_ref[...], 0, rows)
    own_p = column(norm_ref[...], (1 + slab) * rows, rows)
    got_p = column(norm_ref[...], (1 + (slab ^ 1)) * rows, rows)
    write_block(
        a_ref,
        (role_ref[...], pick(got_q_ref[...], got_p_ref[...])),
        (pick(own_q, own_p), pick(got_q, got_p)),
    )
    write_block(
        b_ref,
        (pick(got_p_ref[...], got_q_ref[...]), other_ref[...]),
        (pick(got_p, got_q), pick(own_p, own_q)),
    )


def row_numbers(plan, slab, blk, role, rows, steps, place):
    chip = slab >> 1
    number = place
    for i, step in enumerate(steps):
        for other in (0, 1):
            core = role ^ other
            p_shard = blk * (2 * plan.chip_count) + 2 * peer(chip, step, plan.chip_count) + core
            q_shard = (2 * chip + core) * plan.blk_count + peer(blk, step, plan.blk_count)
            p_base = p_shard * rows if step < plan.chip_count else -(1 << 24)
            q_base = q_shard * rows if step < plan.blk_count else -(1 << 25)
            start = (2 * i + other) * rows
            base = jnp.where(role == 0, p_base, q_base) - start
            number = jnp.where(place >= start, place + base, number)
    return number


def gradient(plan, rows, scalars, a_steps, a_refs, a_norm, b_steps, b_refs):
    slab, blk = (ref[0] for ref in scalars)
    a, b = read_rows(a_refs, rows), read_rows(b_refs, rows)
    scale = 2.0 / math.sqrt(a.shape[1])
    scores = scale * lax.dot_general(
        a, b, (((1,), (1,)), ((), ())), preferred_element_type=jnp.float32
    )
    role = slab & 1
    numbers = functools.partial(row_numbers, plan, slab, blk, rows=rows)
    a_place = lax.broadcasted_iota(jnp.int32, (a.shape[0], 1), 0)
    b_place = lax.broadcasted_iota(jnp.int32, (1, b.shape[0]), 1)
    a_number = numbers(role, steps=a_steps, place=a_place)
    b_number = numbers(1 - role, steps=b_steps, place=b_place)
    weights = (0.5 * scale) * (
        jnp.exp(scores - a_norm)
        + jnp.exp(scores - norm_row(b_refs, rows))
        - 2.0 * (a_number == b_number).astype(jnp.float32)
    )
    high = weights.astype(jnp.bfloat16)
    low = (weights - high.astype(jnp.float32)).astype(jnp.bfloat16)
    return jnp.dot(
        jnp.concatenate([high, low], axis=1),
        jnp.concatenate([b, b], axis=0),
        preferred_element_type=jnp.float32,
    )


def early_kernel(plan, rows, a_steps, b_steps, *refs):
    scalars, refs, (out_ref, norm_ref) = refs[:2], refs[2:-2], refs[-2:]
    a_refs, b_refs = refs[: len(a_steps)], refs[len(a_steps) :]
    a_norm = norm_column(a_refs, rows)
    out_ref[...] = gradient(plan, rows, scalars, a_steps, a_refs, a_norm, b_steps, b_refs)
    norm_ref[...] = jnp.broadcast_to(a_norm, norm_ref.shape)


def late_kernel(plan, rows, a_steps, b_steps, *refs):
    scalars, (early_ref, norm_ref), refs = refs[:2], refs[2:4], refs[4:]
    n = len(a_steps)
    a_refs, b_refs, out_refs = refs[:n], refs[n : n + len(b_steps)], refs[n + len(b_steps) :]
    total = early_ref[...] + gradient(
        plan, rows, scalars, a_steps, a_refs, norm_ref[:, 0:1], b_steps, b_refs
    )
    for i, out_ref in enumerate(out_refs):
        write_partial(out_ref, total[2 * rows * i : 2 * rows * (i + 1)])


def own_kernel(plan, rows, steps, *refs):
    scalars, loss_ref, refs, (out_ref, size_ref) = refs[:2], refs[2], refs[3:-2], refs[-2:]
    a_refs, b_refs = refs[:1], refs[1:]
    a_norm = norm_column(a_refs, rows)
    size_ref[...] = jnp.full(size_ref.shape, loss_ref[0], jnp.float32)
    out_ref[...] = gradient(plan, rows, scalars, steps[:1], a_refs, a_norm, steps, b_refs)


def tiles(block):
    rows, width = block.shape
    return [
        block[:, i : i + LANES].reshape(rows // SIZE_ROWS, SIZE_ROWS, LANES)
        for i in range(0, width, LANES)
    ]


def write_partial(ref, block):
    rows = block.shape[0]
    chunks = tiles(block)
    largest = functools.reduce(
        jnp.maximum, [jnp.max(jnp.abs(chunk), axis=0, keepdims=True) for chunk in chunks]
    )
    power = jnp.ceil(jnp.log2(jnp.maximum(largest, 1e-30))) - 10.0
    factor = jnp.exp2(-power)
    for i, chunk in enumerate(chunks):
        ref[i * rows : (i + 1) * rows] = (chunk * factor).reshape(rows, LANES)
    ref[len(chunks) * rows :] = power[0]


def sum_kernel(loss_ref, own_ref, *refs):
    partial_refs, (keep_ref, give_ref) = refs[:-2], refs[-2:]
    rows, width = own_ref.shape
    tail = rows * (width // LANES)
    loss = loss_ref[...]
    factors = [jnp.exp2(ref[tail:])[None] for ref in partial_refs]
    for i, total in enumerate(tiles(own_ref[...])):
        for ref, factor in zip(partial_refs, factors):
            total = total + tiles(ref[i * rows : (i + 1) * rows])[0] * factor
        total = (total * loss[None]).reshape(rows, LANES)
        keep_ref[:, i * LANES : (i + 1) * LANES] = total[: rows // 2]
        give_ref[:, i * LANES : (i + 1) * LANES] = total[rows // 2 :]


VMEM = pl.BlockSpec(memory_space=pltpu.VMEM)
SMEM = pl.BlockSpec(memory_space=pltpu.SMEM)


def call(kernel, name, scalars, arrays, out_shape, mebibytes, flops=0):
    return pl.pallas_call(
        kernel,
        out_shape=out_shape,
        in_specs=[SMEM] * len(scalars) + [VMEM] * len(arrays),
        out_specs=[VMEM] * len(out_shape),
        name=name,
        compiler_params=pltpu.CompilerParams(vmem_limit_bytes=mebibytes * 1024 * 1024),
        cost_estimate=pl.CostEstimate(flops=flops, bytes_accessed=0, transcendentals=0),
    )(*(x.reshape(1) for x in scalars), *arrays)


def local(plan, queries, passages, query_lognorm, passage_lognorm, loss_cotangent):
    rows, width = queries.shape
    count = plan.group_size
    chunk_rows = 2 * rows * (width // LANES)
    slab = lax.axis_index("slab")
    blk = lax.axis_index("blk")
    core = slab & 1

    def swapped(block):
        return lax.ppermute(block, AXES, plan.core_pairs())

    packed = jax.ShapeDtypeStruct((chunk_rows + NORM_ROWS, LANES), jnp.bfloat16)
    mine, others = call(
        pack_kernel,
        "pack",
        (slab,),
        (
            jnp.where(core == 1, queries, passages),
            jnp.where(core == 1, passages, queries),
            swapped(queries),
            swapped(passages),
            jnp.concatenate([query_lognorm, passage_lognorm]).reshape(1, -1),
            swapped(query_lognorm).reshape(1, -1),
        ),
        [packed, packed],
        4,
    )

    a_parts, b_parts = [mine], [others]
    for step in range(1, count):
        back = [(to, at) for at, to in plan.group_pairs(step)]
        a_parts.append(lax.ppermute(mine, AXES, back))
        b_parts.append(swapped(a_parts[-1]))

    scalars = (slab, blk)
    steps = list(range(count))
    last = steps[1:3]
    soon = [i for i in steps if i not in last]
    a_others = a_parts[1:]
    other_rows = 2 * rows * (count - 1)
    early = call(
        functools.partial(early_kernel, plan, rows, steps[1:], soon),
        "early",
        scalars,
        (*a_others, *(b_parts[i] for i in soon)),
        [
            jax.ShapeDtypeStruct((other_rows, width), jnp.float32),
            jax.ShapeDtypeStruct((other_rows, LANES), jnp.float32),
        ],
        3 * count,
        flops=10**9,
    )
    partials = call(
        functools.partial(late_kernel, plan, rows, steps[1:], last),
        "late",
        scalars,
        (*early, *a_others, *(b_parts[i] for i in last)),
        [jax.ShapeDtypeStruct((chunk_rows + SIZE_ROWS, LANES), jnp.float32)] * (count - 1),
        3 * count,
    )
    own, loss = call(
        functools.partial(own_kernel, plan, rows, steps),
        "own",
        (*scalars, loss_cotangent),
        (mine, *b_parts),
        [
            jax.ShapeDtypeStruct((2 * rows, width), jnp.float32),
            jax.ShapeDtypeStruct((SIZE_ROWS, LANES), jnp.float32),
        ],
        3 * count,
        flops=10**9,
    )
    half = jax.ShapeDtypeStruct((rows, width), jnp.float32)

    arrived = [
        lax.ppermute(x.astype(jnp.float16), AXES, plan.group_pairs(1 + i)).astype(jnp.float32)
        for i, x in enumerate(partials)
    ]
    keep, give = call(sum_kernel, "sum", (), (loss, own, *arrived), [half, half], 2 * count)
    got = swapped(give)
    return jnp.where(core == 1, keep, got), jnp.where(core == 1, got, keep)


def solution(mesh):
    plan = Plan(mesh.shape["slab"], mesh.shape["blk"])
    return jax.shard_map(
        functools.partial(local, plan),
        mesh=mesh,
        in_specs=(
            P(("slab", "blk"), None),
            P(("blk", "slab"), None),
            P(("slab", "blk")),
            P("blk"),
            P(),
        ),
        out_specs=(P(("slab", "blk"), None), P(("blk", "slab"), None)),
        check_vma=False,
    )
```

```python
import functools
import math

import jax
import jax.numpy as jnp
from jax import lax
from jax.experimental import pallas as pl
from jax.experimental.pallas import tpu as pltpu
from jax.sharding import PartitionSpec as P

AXES = ("slab", "blk")
LANES = 128
NORM_ROWS = 16
FIRST_STEPS = ((1, 3, 2), (2, 1, 3))
PIECES = 1
SIZE_ROWS = 8


def peer(index, step, count):
    if count & (count - 1) == 0:
        return index ^ step
    return (index + step) % count


class Plan:
    def __init__(self, slab_count, blk_count):
        self.blk_count = blk_count
        self.chip_count = slab_count // 2
        self.group_size = max(self.chip_count, blk_count)

    def step(self, role, turn):
        steps = FIRST_STEPS[role]
        if turn == 0 or self.group_size <= len(steps):
            return turn
        return steps[turn - 1] if turn <= len(steps) else turn

    def device(self, chip, core, blk):
        return (2 * chip + core) * self.blk_count + blk

    def each(self):
        for chip in range(self.chip_count):
            for blk in range(self.blk_count):
                yield chip, blk

    def core_pairs(self):
        return [
            (self.device(chip, core, blk), self.device(chip, 1 - core, blk))
            for chip, blk in self.each()
            for core in (0, 1)
        ]

    def group_pairs(self, turn, across=False):
        pairs = []
        p_step, q_step = self.step(0, turn), self.step(1, turn)
        for chip, blk in self.each():
            if p_step < self.chip_count:
                other = peer(chip, p_step, self.chip_count)
                pairs.append((self.device(chip, 0, blk), self.device(other, int(across), blk)))
            if q_step < self.blk_count:
                other = peer(blk, q_step, self.blk_count)
                pairs.append((self.device(chip, 1, blk), self.device(chip, 1 - across, other)))
        return pairs


def column(values, first, rows):
    shape = (rows, values.shape[1])
    lane = lax.broadcasted_iota(jnp.int32, shape, 1)
    row = lax.broadcasted_iota(jnp.int32, shape, 0)
    picked = jnp.where(lane == row + first, jnp.broadcast_to(values, shape), 0.0)
    return jnp.sum(picked, axis=1, keepdims=True)


def as_row(values, lanes):
    shape = (values.shape[0], lanes)
    lane = lax.broadcasted_iota(jnp.int32, shape, 1)
    row = lax.broadcasted_iota(jnp.int32, shape, 0)
    picked = jnp.where(lane == row, jnp.broadcast_to(values, shape), 0.0)
    return jnp.sum(picked, axis=0, keepdims=True)


def split_three(values):
    high = values.astype(jnp.bfloat16).astype(jnp.float32)
    middle = (values - high).astype(jnp.bfloat16).astype(jnp.float32)
    return high, middle, values - high - middle


def write_block(out_ref, halves, norms):
    rows, width = halves[0].shape
    for chunk in range(width // LANES):
        for half in (0, 1):
            start = (2 * chunk + half) * rows
            out_ref[start : start + rows] = halves[half][:, chunk * LANES : (chunk + 1) * LANES]
    shape = (NORM_ROWS, LANES)
    row = lax.broadcasted_iota(jnp.int32, shape, 0)
    tail = jnp.zeros(shape, jnp.float32)
    for half in (0, 1):
        for i, part in enumerate(split_three(as_row(norms[half], LANES))):
            tail = jnp.where(row == 3 * half + i, jnp.broadcast_to(part, shape), tail)
    out_ref[2 * rows * (width // LANES) :] = tail.astype(jnp.bfloat16)


def read_rows(refs, rows):
    size = 2 * rows
    chunks = (refs[0].shape[0] - NORM_ROWS) // size
    parts = [[ref[size * i : size * (i + 1)] for i in range(chunks)] for ref in refs]
    return jnp.concatenate([jnp.concatenate(part, axis=1) for part in parts], axis=0)


def read_norms(refs):
    norms = []
    for ref in refs:
        tail = ref[ref.shape[0] - NORM_ROWS :].astype(jnp.float32)
        norms += [tail[i : i + 1] + tail[i + 1 : i + 2] + tail[i + 2 : i + 3] for i in (0, 3)]
    return norms


def norm_column(refs, rows):
    return jnp.concatenate([column(norm, 0, rows) for norm in read_norms(refs)], axis=0)


def norm_row(refs, rows):
    norms, per_row = read_norms(refs), LANES // rows
    lane = lax.broadcasted_iota(jnp.int32, (1, LANES), 1)
    pieces = []
    for start in range(0, len(norms), per_row):
        piece = norms[start]
        for i, norm in enumerate(norms[start + 1 : start + per_row], 1):
            piece = jnp.where(lane >= i * rows, pltpu.roll(norm, i * rows, 1), piece)
        pieces.append(piece)
    return jnp.concatenate(pieces, axis=1)[:, : len(norms) * rows]


def pack_kernel(
    slab_ref, role_ref, other_ref, got_q_ref, got_p_ref, norm_ref, got_norm_ref, a_ref, b_ref
):
    rows = role_ref.shape[0]
    slab = slab_ref[0]
    pick = functools.partial(jnp.where, (slab & 1) == 1)
    own_q = column(norm_ref[...], 0, rows)
    got_q = column(got_norm_ref[...], 0, rows)
    own_p = column(norm_ref[...], (1 + slab) * rows, rows)
    got_p = column(norm_ref[...], (1 + (slab ^ 1)) * rows, rows)
    write_block(
        a_ref,
        (role_ref[...], pick(got_q_ref[...], got_p_ref[...])),
        (pick(own_q, own_p), pick(got_q, got_p)),
    )
    write_block(
        b_ref,
        (pick(got_p_ref[...], got_q_ref[...]), other_ref[...]),
        (pick(got_p, got_q), pick(own_p, own_q)),
    )


def row_numbers(plan, slab, blk, role, rows, turns, place):
    chip = slab >> 1
    number = place
    for i, turn in enumerate(turns):
        p_step, q_step = plan.step(0, turn), plan.step(1, turn)
        for other in (0, 1):
            core = role ^ other
            p_shard = blk * (2 * plan.chip_count) + 2 * peer(chip, p_step, plan.chip_count) + core
            q_shard = (2 * chip + core) * plan.blk_count + peer(blk, q_step, plan.blk_count)
            p_base = p_shard * rows if p_step < plan.chip_count else -(1 << 24)
            q_base = q_shard * rows if q_step < plan.blk_count else -(1 << 25)
            start = (2 * i + other) * rows
            base = jnp.where(role == 0, p_base, q_base) - start
            number = jnp.where(place >= start, place + base, number)
    return number


def gradient(plan, rows, scalars, a_turns, a_refs, a_norm, b_turns, b_refs):
    slab, blk = (ref[0] for ref in scalars)
    a, b = read_rows(a_refs, rows), read_rows(b_refs, rows)
    scale = 2.0 / math.sqrt(a.shape[1])
    scores = scale * lax.dot_general(
        a, b, (((1,), (1,)), ((), ())), preferred_element_type=jnp.float32
    )
    role = slab & 1
    numbers = functools.partial(row_numbers, plan, slab, blk, rows=rows)
    a_place = lax.broadcasted_iota(jnp.int32, (a.shape[0], 1), 0)
    b_place = lax.broadcasted_iota(jnp.int32, (1, b.shape[0]), 1)
    a_number = numbers(role, turns=a_turns, place=a_place)
    b_number = numbers(1 - role, turns=b_turns, place=b_place)
    weights = (0.5 * scale) * (
        jnp.exp(scores - a_norm)
        + jnp.exp(scores - norm_row(b_refs, rows))
        - 2.0 * (a_number == b_number).astype(jnp.float32)
    )
    high = weights.astype(jnp.bfloat16)
    low = (weights - high.astype(jnp.float32)).astype(jnp.bfloat16)
    return jnp.dot(
        jnp.concatenate([high, low], axis=1),
        jnp.concatenate([b, b], axis=0),
        preferred_element_type=jnp.float32,
    )


def early_kernel(plan, rows, a_turns, b_turns, *refs):
    scalars, refs, (out_ref, norm_ref) = refs[:2], refs[3:-2], refs[-2:]
    a_refs, b_refs = refs[: len(a_turns)], refs[len(a_turns) :]
    a_norm = norm_column(a_refs, rows)
    out_ref[...] = gradient(plan, rows, scalars, a_turns, a_refs, a_norm, b_turns, b_refs)
    norm_ref[...] = jnp.broadcast_to(a_norm, norm_ref.shape)


def late_kernel(plan, rows, a_turns, b_turns, *refs):
    scalars, (early_ref, norm_ref), refs = refs[:2], refs[2:4], refs[4:]
    n = len(a_turns)
    a_refs, b_refs, out_refs = refs[:n], refs[n : n + len(b_turns)], refs[n + len(b_turns) :]
    total = early_ref[...] + gradient(
        plan, rows, scalars, a_turns, a_refs, norm_ref[:, 0:1], b_turns, b_refs
    )
    write_partial(out_refs[0], total[:rows])
    write_partial(out_refs[1], total[rows : 2 * rows])
    for i, out_ref in enumerate(out_refs[2:], 1):
        write_partial(out_ref, total[2 * rows * i : 2 * rows * (i + 1)])


def own_kernel(plan, rows, turns, *refs):
    scalars, a_refs, b_refs, out_ref = refs[:2], refs[2:3], refs[3:-1], refs[-1]
    a_norm = norm_column(a_refs, rows)
    out_ref[...] = gradient(plan, rows, scalars, turns[:1], a_refs, a_norm, turns, b_refs)


def tiles(block):
    rows, width = block.shape
    return [
        block[:, i : i + LANES].reshape(rows // SIZE_ROWS, SIZE_ROWS, LANES)
        for i in range(0, width, LANES)
    ]


def write_partial(ref, block):
    rows = block.shape[0]
    chunks = tiles(block)
    largest = functools.reduce(
        jnp.maximum, [jnp.max(jnp.abs(chunk), axis=0, keepdims=True) for chunk in chunks]
    )
    power = jnp.ceil(jnp.log2(jnp.maximum(largest, 1e-30))) - 10.0
    factor = jnp.exp2(-power)
    for i, chunk in enumerate(chunks):
        ref[i * rows : (i + 1) * rows] = (chunk * factor).reshape(rows, LANES)
    ref[len(chunks) * rows :] = power[0]


def spread_kernel(value_ref, out_ref):
    out_ref[...] = jnp.full(out_ref.shape, value_ref[0], jnp.float32)


def sum_kernel(loss_ref, own_ref, *refs):
    partial_refs, (keep_ref, *give_refs) = refs[: -1 - PIECES], refs[-1 - PIECES :]
    rows, width = own_ref.shape
    tail = rows * (width // LANES)
    loss = loss_ref[...]
    factors = [jnp.exp2(ref[tail:])[None] for ref in partial_refs]
    gives = []
    for i, total in enumerate(tiles(own_ref[...])):
        for ref, factor in zip(partial_refs, factors):
            total = total + tiles(ref[i * rows : (i + 1) * rows])[0] * factor
        total = (total * loss[None]).reshape(rows, LANES)
        keep_ref[:, i * LANES : (i + 1) * LANES] = total[: rows // 2]
        gives.append(total[rows // 2 :])
    size = rows // 2 // PIECES
    for i, give_ref in enumerate(give_refs):
        write_partial(
            give_ref, jnp.concatenate([give[i * size : (i + 1) * size] for give in gives], axis=1)
        )


def end_kernel(loss_ref, keep_ref, *refs):
    got_refs, last_refs, (keep_out, got_out) = refs[:PIECES], refs[PIECES:-2], refs[-2:]
    rows, width = keep_ref.shape
    tail, size = rows * (width // LANES), rows // PIECES
    loss = loss_ref[...]
    factors = [(jnp.exp2(ref[tail:]) * loss)[None] for ref in last_refs]
    got_factors = [jnp.exp2(ref[size * (width // LANES) :])[None] for ref in got_refs]
    for i, keep in enumerate(tiles(keep_ref[...])):
        lanes = slice(i * LANES, (i + 1) * LANES)
        got = jnp.concatenate(
            [
                tiles(ref[i * size : (i + 1) * size])[0] * factor
                for ref, factor in zip(got_refs, got_factors)
            ],
            axis=0,
        )
        for total, ref, factor, out_ref in zip((keep, got), last_refs, factors, (keep_out, got_out)):
            total = total + tiles(ref[i * rows : (i + 1) * rows])[0] * factor
            out_ref[:, lanes] = total.reshape(rows, LANES)


VMEM = pl.BlockSpec(memory_space=pltpu.VMEM)
SMEM = pl.BlockSpec(memory_space=pltpu.SMEM)


def call(kernel, name, scalars, arrays, out_shape, mebibytes, flops=0):
    return pl.pallas_call(
        kernel,
        out_shape=out_shape,
        in_specs=[SMEM] * len(scalars) + [VMEM] * len(arrays),
        out_specs=[VMEM] * len(out_shape),
        name=name,
        compiler_params=pltpu.CompilerParams(vmem_limit_bytes=mebibytes * 1024 * 1024),
        cost_estimate=pl.CostEstimate(flops=flops, bytes_accessed=0, transcendentals=0),
    )(*(x.reshape(1) for x in scalars), *arrays)


def local(plan, queries, passages, query_lognorm, passage_lognorm, loss_cotangent):
    rows, width = queries.shape
    count = plan.group_size
    chunk_rows = 2 * rows * (width // LANES)
    slab = lax.axis_index("slab")
    blk = lax.axis_index("blk")
    core = slab & 1

    def swapped(block):
        return lax.ppermute(block, AXES, plan.core_pairs())

    packed = jax.ShapeDtypeStruct((chunk_rows + NORM_ROWS, LANES), jnp.bfloat16)
    mine, others = call(
        pack_kernel,
        "pack",
        (slab,),
        (
            jnp.where(core == 1, queries, passages),
            jnp.where(core == 1, passages, queries),
            swapped(queries),
            swapped(passages),
            jnp.concatenate([query_lognorm, passage_lognorm]).reshape(1, -1),
            swapped(query_lognorm).reshape(1, -1),
        ),
        [packed, packed],
        4,
    )

    (loss,) = call(
        spread_kernel,
        "spread",
        (loss_cotangent,),
        (),
        [jax.ShapeDtypeStruct((SIZE_ROWS, LANES), jnp.float32)],
        1,
        flops=10**9,
    )

    a_parts, b_parts = [mine], [others]
    for turn in range(1, count):
        back = [(to, at) for at, to in plan.group_pairs(turn)]
        a_parts.append(lax.ppermute(mine, AXES, back))
        b_parts.append(swapped(a_parts[-1]))

    scalars = (slab, blk)
    turns = list(range(count))
    last = turns[1:3]
    soon = [i for i in turns if i not in last]
    a_others = a_parts[1:]
    other_rows = 2 * rows * (count - 1)
    early = call(
        functools.partial(early_kernel, plan, rows, turns[1:], soon),
        "early",
        scalars,
        (loss, *a_others, *(b_parts[i] for i in soon)),
        [
            jax.ShapeDtypeStruct((other_rows, width), jnp.float32),
            jax.ShapeDtypeStruct((other_rows, LANES), jnp.float32),
        ],
        3 * count,
        flops=10**9,
    )
    partials = call(
        functools.partial(late_kernel, plan, rows, turns[1:], last),
        "late",
        scalars,
        (*early, *a_others, *(b_parts[i] for i in last)),
        [jax.ShapeDtypeStruct((chunk_rows // 2 + SIZE_ROWS, LANES), jnp.float32)] * 2
        + [jax.ShapeDtypeStruct((chunk_rows + SIZE_ROWS, LANES), jnp.float32)] * (count - 2),
        3 * count,
    )
    (own,) = call(
        functools.partial(own_kernel, plan, rows, turns),
        "own",
        scalars,
        (mine, *b_parts),
        [jax.ShapeDtypeStruct((2 * rows, width), jnp.float32)],
        3 * count,
        flops=10**9,
    )
    half = jax.ShapeDtypeStruct((rows, width), jnp.float32)

    def crossed(partial, turn, across=False):
        pairs = plan.group_pairs(turn, across)
        return lax.ppermute(partial.astype(jnp.float16), AXES, pairs).astype(jnp.float32)

    arrived = [crossed(x, turn) for turn, x in enumerate(partials[2:], 2)]
    last = [crossed(partials[0], 1), crossed(partials[1], 1, True)]
    piece = jax.ShapeDtypeStruct((chunk_rows // 2 // PIECES + SIZE_ROWS, LANES), jnp.float32)
    keep, *gives = call(
        sum_kernel, "sum", (), (loss, own, *arrived), [half] + [piece] * PIECES, 2 * count
    )
    gots = [swapped(give.astype(jnp.float16)).astype(jnp.float32) for give in gives]
    keep, got = call(end_kernel, "end", (), (loss, keep, *gots, *last), [half, half], 4)
    return jnp.where(core == 1, keep, got), jnp.where(core == 1, got, keep)


def solution(mesh):
    plan = Plan(mesh.shape["slab"], mesh.shape["blk"])
    return jax.shard_map(
        functools.partial(local, plan),
        mesh=mesh,
        in_specs=(
            P(("slab", "blk"), None),
            P(("blk", "slab"), None),
            P(("slab", "blk")),
            P("blk"),
            P(),
        ),
        out_specs=(P(("slab", "blk"), None), P(("blk", "slab"), None)),
        check_vma=False,
    )
```

```python
import functools
import math

import jax
import jax.numpy as jnp
from jax import lax
from jax.experimental import pallas as pl
from jax.experimental.pallas import tpu as pltpu
from jax.sharding import PartitionSpec as P

AXES = ("slab", "blk")
LANES = 128
NORM_ROWS = 16
FIRST_STEPS = ((1, 2, 3), (1, 2, 3))
SIZE_ROWS = 8


def peer(index, step, count):
    if count & (count - 1) == 0:
        return index ^ step
    return (index + step) % count


class Plan:
    def __init__(self, slab_count, blk_count):
        self.blk_count = blk_count
        self.chip_count = slab_count // 2
        self.group_size = max(self.chip_count, blk_count)

    def step(self, role, turn):
        steps = FIRST_STEPS[role]
        if turn == 0 or self.group_size <= len(steps):
            return turn
        return steps[turn - 1] if turn <= len(steps) else turn

    def device(self, chip, core, blk):
        return (2 * chip + core) * self.blk_count + blk

    def each(self):
        for chip in range(self.chip_count):
            for blk in range(self.blk_count):
                yield chip, blk

    def core_pairs(self):
        return [
            (self.device(chip, core, blk), self.device(chip, 1 - core, blk))
            for chip, blk in self.each()
            for core in (0, 1)
        ]

    def group_pairs(self, turn, across=False):
        pairs = []
        p_step, q_step = self.step(0, turn), self.step(1, turn)
        for chip, blk in self.each():
            if p_step < self.chip_count:
                other = peer(chip, p_step, self.chip_count)
                pairs.append((self.device(chip, 0, blk), self.device(other, int(across), blk)))
            if q_step < self.blk_count:
                other = peer(blk, q_step, self.blk_count)
                pairs.append((self.device(chip, 1, blk), self.device(chip, 1 - across, other)))
        return pairs


def column(values, first, rows):
    shape = (rows, values.shape[1])
    lane = lax.broadcasted_iota(jnp.int32, shape, 1)
    row = lax.broadcasted_iota(jnp.int32, shape, 0)
    picked = jnp.where(lane == row + first, jnp.broadcast_to(values, shape), 0.0)
    return jnp.sum(picked, axis=1, keepdims=True)


def as_row(values, lanes):
    shape = (values.shape[0], lanes)
    lane = lax.broadcasted_iota(jnp.int32, shape, 1)
    row = lax.broadcasted_iota(jnp.int32, shape, 0)
    picked = jnp.where(lane == row, jnp.broadcast_to(values, shape), 0.0)
    return jnp.sum(picked, axis=0, keepdims=True)


def split_three(values):
    high = values.astype(jnp.bfloat16).astype(jnp.float32)
    middle = (values - high).astype(jnp.bfloat16).astype(jnp.float32)
    return high, middle, values - high - middle


def write_block(out_ref, halves, norms):
    rows, width = halves[0].shape
    for chunk in range(width // LANES):
        for half in (0, 1):
            start = (2 * chunk + half) * rows
            out_ref[start : start + rows] = halves[half][:, chunk * LANES : (chunk + 1) * LANES]
    shape = (NORM_ROWS, LANES)
    row = lax.broadcasted_iota(jnp.int32, shape, 0)
    tail = jnp.zeros(shape, jnp.float32)
    for half in (0, 1):
        for i, part in enumerate(split_three(as_row(norms[half], LANES))):
            tail = jnp.where(row == 3 * half + i, jnp.broadcast_to(part, shape), tail)
    out_ref[2 * rows * (width // LANES) :] = tail.astype(jnp.bfloat16)


def read_rows(refs, rows):
    size = 2 * rows
    chunks = (refs[0].shape[0] - NORM_ROWS) // size
    parts = [[ref[size * i : size * (i + 1)] for i in range(chunks)] for ref in refs]
    return jnp.concatenate([jnp.concatenate(part, axis=1) for part in parts], axis=0)


def read_norms(refs):
    norms = []
    for ref in refs:
        tail = ref[ref.shape[0] - NORM_ROWS :].astype(jnp.float32)
        norms += [tail[i : i + 1] + tail[i + 1 : i + 2] + tail[i + 2 : i + 3] for i in (0, 3)]
    return norms


def norm_column(refs, rows):
    return jnp.concatenate([column(norm, 0, rows) for norm in read_norms(refs)], axis=0)


def norm_row(refs, rows):
    norms, per_row = read_norms(refs), LANES // rows
    lane = lax.broadcasted_iota(jnp.int32, (1, LANES), 1)
    pieces = []
    for start in range(0, len(norms), per_row):
        piece = norms[start]
        for i, norm in enumerate(norms[start + 1 : start + per_row], 1):
            piece = jnp.where(lane >= i * rows, pltpu.roll(norm, i * rows, 1), piece)
        pieces.append(piece)
    return jnp.concatenate(pieces, axis=1)[:, : len(norms) * rows]


def pack_kernel(
    slab_ref, role_ref, other_ref, got_q_ref, got_p_ref, norm_ref, got_norm_ref, a_ref, b_ref
):
    rows = role_ref.shape[0]
    slab = slab_ref[0]
    pick = functools.partial(jnp.where, (slab & 1) == 1)
    own_q = column(norm_ref[...], 0, rows)
    got_q = column(got_norm_ref[...], 0, rows)
    own_p = column(norm_ref[...], (1 + slab) * rows, rows)
    got_p = column(norm_ref[...], (1 + (slab ^ 1)) * rows, rows)
    write_block(
        a_ref,
        (role_ref[...], pick(got_q_ref[...], got_p_ref[...])),
        (pick(own_q, own_p), pick(got_q, got_p)),
    )
    write_block(
        b_ref,
        (pick(got_p_ref[...], got_q_ref[...]), other_ref[...]),
        (pick(got_p, got_q), pick(own_p, own_q)),
    )


def row_numbers(plan, slab, blk, role, rows, turns, place):
    chip = slab >> 1
    number = place
    for i, turn in enumerate(turns):
        p_step, q_step = plan.step(0, turn), plan.step(1, turn)
        for other in (0, 1):
            core = role ^ other
            p_shard = blk * (2 * plan.chip_count) + 2 * peer(chip, p_step, plan.chip_count) + core
            q_shard = (2 * chip + core) * plan.blk_count + peer(blk, q_step, plan.blk_count)
            p_base = p_shard * rows if p_step < plan.chip_count else -(1 << 24)
            q_base = q_shard * rows if q_step < plan.blk_count else -(1 << 25)
            start = (2 * i + other) * rows
            base = jnp.where(role == 0, p_base, q_base) - start
            number = jnp.where(place >= start, place + base, number)
    return number


def gradient(plan, rows, scalars, a_turns, a_refs, a_norm, b_turns, b_refs):
    slab, blk = (ref[0] for ref in scalars)
    a, b = read_rows(a_refs, rows), read_rows(b_refs, rows)
    scale = 2.0 / math.sqrt(a.shape[1])
    scores = scale * lax.dot_general(
        a, b, (((1,), (1,)), ((), ())), preferred_element_type=jnp.float32
    )
    role = slab & 1
    numbers = functools.partial(row_numbers, plan, slab, blk, rows=rows)
    a_place = lax.broadcasted_iota(jnp.int32, (a.shape[0], 1), 0)
    b_place = lax.broadcasted_iota(jnp.int32, (1, b.shape[0]), 1)
    a_number = numbers(role, turns=a_turns, place=a_place)
    b_number = numbers(1 - role, turns=b_turns, place=b_place)
    weights = (0.5 * scale) * (
        jnp.exp(scores - a_norm)
        + jnp.exp(scores - norm_row(b_refs, rows))
        - 2.0 * (a_number == b_number).astype(jnp.float32)
    )
    high = weights.astype(jnp.bfloat16)
    low = (weights - high.astype(jnp.float32)).astype(jnp.bfloat16)
    if b.shape[0] >= 256:
        both = jnp.dot(jnp.concatenate([high, low], axis=0), b, preferred_element_type=jnp.float32)
        return both[: a.shape[0]] + both[a.shape[0] :]
    return jnp.dot(
        jnp.concatenate([high, low], axis=1),
        jnp.concatenate([b, b], axis=0),
        preferred_element_type=jnp.float32,
    )


def early_kernel(plan, rows, a_turns, b_turns, *refs):
    scalars, refs, (out_ref, norm_ref) = refs[:2], refs[3:-2], refs[-2:]
    a_refs, b_refs = refs[: len(a_turns)], refs[len(a_turns) :]
    a_norm = norm_column(a_refs, rows)
    out_ref[...] = gradient(plan, rows, scalars, a_turns, a_refs, a_norm, b_turns, b_refs)
    norm_ref[...] = jnp.broadcast_to(a_norm, norm_ref.shape)


def late_kernel(plan, rows, a_turns, b_turns, *refs):
    scalars, (early_ref, norm_ref), refs = refs[:2], refs[2:4], refs[4:]
    n = len(a_turns)
    a_refs, b_refs, out_refs = refs[:n], refs[n : n + len(b_turns)], refs[n + len(b_turns) :]
    total = early_ref[...] + gradient(
        plan, rows, scalars, a_turns, a_refs, norm_ref[:, 0:1], b_turns, b_refs
    )
    write_partial(out_refs[0], total[:rows])
    write_partial(out_refs[1], total[rows : 2 * rows])
    for i, out_ref in enumerate(out_refs[2:], 1):
        write_partial(out_ref, total[2 * rows * i : 2 * rows * (i + 1)], 2)


def own_kernel(plan, rows, turns, *refs):
    scalars, a_refs, b_refs, out_ref = refs[:2], refs[2:3], refs[3:-1], refs[-1]
    a_norm = norm_column(a_refs, rows)
    out_ref[...] = gradient(plan, rows, scalars, turns[:1], a_refs, a_norm, turns, b_refs)


def tiles(block):
    rows, width = block.shape
    return [
        block[:, i : i + LANES].reshape(rows // SIZE_ROWS, SIZE_ROWS, LANES)
        for i in range(0, width, LANES)
    ]


def write_partial(ref, block, parts=1):
    size = block.shape[0] // parts
    chunks = tiles(block)
    largest = functools.reduce(
        jnp.maximum, [jnp.max(jnp.abs(chunk), axis=0, keepdims=True) for chunk in chunks]
    )
    power = jnp.ceil(jnp.log2(jnp.maximum(largest, 1e-30))) - 10.0
    factor = jnp.exp2(-power)
    for i, chunk in enumerate(chunks):
        chunk = (chunk * factor).reshape(block.shape[0], LANES)
        for j in range(parts):
            start = (j * len(chunks) + i) * size
            ref[start : start + size] = chunk[j * size : (j + 1) * size]
    start = len(chunks) * block.shape[0]
    copies = (ref.shape[0] - start) // SIZE_ROWS
    ref[start:] = jnp.concatenate([power[0]] * copies, axis=0)


def spread_kernel(value_ref, out_ref):
    out_ref[...] = jnp.full(out_ref.shape, value_ref[0], jnp.float32)


def read_partials(refs, rows, start):
    factors = [jnp.exp2(ref[ref.shape[0] - SIZE_ROWS :])[None] for ref in refs]
    chunks = (refs[0].shape[0] - SIZE_ROWS - start) // rows
    for i in range(chunks):
        yield sum(
            ref[start + i * rows : start + (i + 1) * rows].reshape(-1, SIZE_ROWS, LANES) * factor
            for ref, factor in zip(refs, factors)
        )


def sum_kernel(own_ref, *refs):
    partial_refs, (keep_ref, give_ref) = refs[:-2], refs[-2:]
    rows, width = own_ref.shape
    half = rows // 2
    chunks = width // LANES
    own = tiles(own_ref[...])
    gives = []
    first = [0.0] * chunks
    second = [0.0] * chunks
    if partial_refs:
        both = list(read_partials(partial_refs, half, 0))
        first, second = both[:chunks], both[chunks:]
    for i, total in enumerate(own):
        n = half // SIZE_ROWS
        keep_ref[:, i * LANES : (i + 1) * LANES] = (total[:n] + first[i]).reshape(half, LANES)
        gives.append((total[n:] + second[i]).reshape(half, LANES))
    write_partial(give_ref, jnp.concatenate(gives, axis=1))


def end_kernel(loss_ref, keep_ref, here_ref, got_ref, there_ref, *refs):
    last_refs, (keep_out, got_out) = refs[:-2], refs[-2:]
    rows, width = keep_ref.shape
    loss = loss_ref[...][None]
    here = read_partials([here_ref], rows, 0)
    keeps = read_partials([last_refs[0]], rows, 0)
    gots = read_partials([got_ref, there_ref, last_refs[1]], rows, 0)
    for i, (keep, a, b, got) in enumerate(zip(tiles(keep_ref[...]), here, keeps, gots)):
        lanes = slice(i * LANES, (i + 1) * LANES)
        keep_out[:, lanes] = ((keep + a + b) * loss).reshape(rows, LANES)
        got_out[:, lanes] = (got * loss).reshape(rows, LANES)


VMEM = pl.BlockSpec(memory_space=pltpu.VMEM)
SMEM = pl.BlockSpec(memory_space=pltpu.SMEM)


def call(kernel, name, scalars, arrays, out_shape, mebibytes, flops=0):
    return pl.pallas_call(
        kernel,
        out_shape=out_shape,
        in_specs=[SMEM] * len(scalars) + [VMEM] * len(arrays),
        out_specs=[VMEM] * len(out_shape),
        name=name,
        compiler_params=pltpu.CompilerParams(vmem_limit_bytes=mebibytes * 1024 * 1024),
        cost_estimate=pl.CostEstimate(flops=flops, bytes_accessed=0, transcendentals=0),
    )(*(x.reshape(1) for x in scalars), *arrays)


def local(plan, queries, passages, query_lognorm, passage_lognorm, loss_cotangent):
    rows, width = queries.shape
    count = plan.group_size
    chunk_rows = 2 * rows * (width // LANES)
    slab = lax.axis_index("slab")
    blk = lax.axis_index("blk")
    core = slab & 1

    def swapped(block):
        return lax.ppermute(block, AXES, plan.core_pairs())

    packed = jax.ShapeDtypeStruct((chunk_rows + NORM_ROWS, LANES), jnp.bfloat16)
    mine, others = call(
        pack_kernel,
        "pack",
        (slab,),
        (
            jnp.where(core == 1, queries, passages),
            jnp.where(core == 1, passages, queries),
            swapped(queries),
            swapped(passages),
            jnp.concatenate([query_lognorm, passage_lognorm]).reshape(1, -1),
            swapped(query_lognorm).reshape(1, -1),
        ),
        [packed, packed],
        4,
    )

    (loss,) = call(
        spread_kernel,
        "spread",
        (loss_cotangent,),
        (),
        [jax.ShapeDtypeStruct((SIZE_ROWS, LANES), jnp.float32)],
        1,
        flops=10**9,
    )

    a_parts, b_parts = [mine], [others]
    for turn in range(1, count):
        back = [(to, at) for at, to in plan.group_pairs(turn)]
        a_parts.append(lax.ppermute(mine, AXES, back))
        b_parts.append(swapped(a_parts[-1]))

    scalars = (slab, blk)
    turns = list(range(count))
    last = turns[1:3]
    soon = [i for i in turns if i not in last]
    a_others = a_parts[1:]
    other_rows = 2 * rows * (count - 1)
    early = call(
        functools.partial(early_kernel, plan, rows, turns[1:], soon),
        "early",
        scalars,
        (loss, *a_others, *(b_parts[i] for i in soon)),
        [
            jax.ShapeDtypeStruct((other_rows, width), jnp.float32),
            jax.ShapeDtypeStruct((other_rows, LANES), jnp.float32),
        ],
        3 * count,
        flops=10**9,
    )
    partials = call(
        functools.partial(late_kernel, plan, rows, turns[1:], last),
        "late",
        scalars,
        (*early, *a_others, *(b_parts[i] for i in last)),
        [
            jax.ShapeDtypeStruct((chunk_rows // 2 + n * SIZE_ROWS, LANES), jnp.float32)
            for n in (1, 3)
        ]
        + [jax.ShapeDtypeStruct((chunk_rows + SIZE_ROWS, LANES), jnp.float32)] * (count - 2),
        3 * count,
    )
    (own,) = call(
        functools.partial(own_kernel, plan, rows, turns),
        "own",
        scalars,
        (mine, *b_parts),
        [jax.ShapeDtypeStruct((2 * rows, width), jnp.float32)],
        3 * count,
        flops=10**9,
    )
    half = jax.ShapeDtypeStruct((rows, width), jnp.float32)

    def crossed(partial, turn, across=False):
        return lax.ppermute(partial.astype(jnp.float16), AXES, plan.group_pairs(turn, across))

    def wide(block):
        return block.astype(jnp.float32)

    arrived = [crossed(x, turn) for turn, x in enumerate(partials[2:], 2)]
    last = [wide(crossed(partials[0], 1)), wide(crossed(partials[1], 1, True))]
    piece = jax.ShapeDtypeStruct((chunk_rows // 2 + SIZE_ROWS, LANES), jnp.float32)
    keep, give = call(
        sum_kernel, "sum", (), (own, *(wide(x) for x in arrived[1:])), [half, piece], 2 * count
    )
    got = wide(swapped(give.astype(jnp.float16)))
    there = wide(swapped(arrived[0][chunk_rows // 2 :]))
    keep, got = call(
        end_kernel, "end", (), (loss, keep, wide(arrived[0]), got, there, *last), [half, half], 4
    )
    return jnp.where(core == 1, keep, got), jnp.where(core == 1, got, keep)


def solution(mesh):
    plan = Plan(mesh.shape["slab"], mesh.shape["blk"])
    return jax.shard_map(
        functools.partial(local, plan),
        mesh=mesh,
        in_specs=(
            P(("slab", "blk"), None),
            P(("blk", "slab"), None),
            P(("slab", "blk")),
            P("blk"),
            P(),
        ),
        out_specs=(P(("slab", "blk"), None), P(("blk", "slab"), None)),
        check_vma=False,
    )
```

```python
import functools
import math

import jax
import jax.numpy as jnp
from jax import lax
from jax.experimental import pallas as pl
from jax.experimental.pallas import tpu as pltpu
from jax.sharding import PartitionSpec as P

AXES = ("slab", "blk")
LANES = 128
NORM_ROWS = 16
SIZE_ROWS = 8


def peer(index, step, count):
    if count & (count - 1) == 0:
        return index ^ step
    return (index + step) % count


class Plan:
    def __init__(self, slab_count, blk_count):
        self.blk_count = blk_count
        self.chip_count = slab_count // 2
        self.group_size = max(self.chip_count, blk_count)

    def device(self, chip, core, blk):
        return (2 * chip + core) * self.blk_count + blk

    def each(self):
        for chip in range(self.chip_count):
            for blk in range(self.blk_count):
                yield chip, blk

    def core_pairs(self):
        return [
            (self.device(chip, core, blk), self.device(chip, 1 - core, blk))
            for chip, blk in self.each()
            for core in (0, 1)
        ]

    def group_pairs(self, turn, across=False):
        pairs = []
        for chip, blk in self.each():
            if turn < self.chip_count:
                other = peer(chip, turn, self.chip_count)
                pairs.append((self.device(chip, 0, blk), self.device(other, int(across), blk)))
            if turn < self.blk_count:
                other = peer(blk, turn, self.blk_count)
                pairs.append((self.device(chip, 1, blk), self.device(chip, 1 - across, other)))
        return pairs


def column(values, first, rows):
    shape = (rows, values.shape[1])
    lane = lax.broadcasted_iota(jnp.int32, shape, 1)
    row = lax.broadcasted_iota(jnp.int32, shape, 0)
    picked = jnp.where(lane == row + first, jnp.broadcast_to(values, shape), 0.0)
    return jnp.sum(picked, axis=1, keepdims=True)


def as_row(values, lanes):
    shape = (values.shape[0], lanes)
    lane = lax.broadcasted_iota(jnp.int32, shape, 1)
    row = lax.broadcasted_iota(jnp.int32, shape, 0)
    picked = jnp.where(lane == row, jnp.broadcast_to(values, shape), 0.0)
    return jnp.sum(picked, axis=0, keepdims=True)


def split_three(values):
    high = values.astype(jnp.bfloat16).astype(jnp.float32)
    middle = (values - high).astype(jnp.bfloat16).astype(jnp.float32)
    return high, middle, values - high - middle


def write_block(out_ref, halves, norms):
    rows, width = halves[0].shape
    for chunk in range(width // LANES):
        for half in (0, 1):
            start = (2 * chunk + half) * rows
            out_ref[start : start + rows] = halves[half][:, chunk * LANES : (chunk + 1) * LANES]
    shape = (NORM_ROWS, LANES)
    row = lax.broadcasted_iota(jnp.int32, shape, 0)
    tail = jnp.zeros(shape, jnp.float32)
    for half in (0, 1):
        for i, part in enumerate(split_three(as_row(norms[half], LANES))):
            tail = jnp.where(row == 3 * half + i, jnp.broadcast_to(part, shape), tail)
    out_ref[2 * rows * (width // LANES) :] = tail.astype(jnp.bfloat16)


def read_rows(refs, rows):
    size = 2 * rows
    chunks = (refs[0].shape[0] - NORM_ROWS) // size
    parts = [[ref[size * i : size * (i + 1)] for i in range(chunks)] for ref in refs]
    return jnp.concatenate([jnp.concatenate(part, axis=1) for part in parts], axis=0)


def read_norms(refs):
    norms = []
    for ref in refs:
        tail = ref[ref.shape[0] - NORM_ROWS :].astype(jnp.float32)
        norms += [tail[i : i + 1] + tail[i + 1 : i + 2] + tail[i + 2 : i + 3] for i in (0, 3)]
    return norms


def norm_column(refs, rows):
    return jnp.concatenate([column(norm, 0, rows) for norm in read_norms(refs)], axis=0)


def norm_row(refs, rows):
    norms, per_row = read_norms(refs), LANES // rows
    lane = lax.broadcasted_iota(jnp.int32, (1, LANES), 1)
    pieces = []
    for start in range(0, len(norms), per_row):
        piece = norms[start]
        for i, norm in enumerate(norms[start + 1 : start + per_row], 1):
            piece = jnp.where(lane >= i * rows, pltpu.roll(norm, i * rows, 1), piece)
        pieces.append(piece)
    return jnp.concatenate(pieces, axis=1)[:, : len(norms) * rows]


def pack_kernel(
    slab_ref, role_ref, other_ref, got_q_ref, got_p_ref, norm_ref, got_norm_ref, a_ref, b_ref
):
    rows = role_ref.shape[0]
    slab = slab_ref[0]
    pick = functools.partial(jnp.where, (slab & 1) == 1)
    own_q = column(norm_ref[...], 0, rows)
    got_q = column(got_norm_ref[...], 0, rows)
    own_p = column(norm_ref[...], (1 + slab) * rows, rows)
    got_p = column(norm_ref[...], (1 + (slab ^ 1)) * rows, rows)
    write_block(
        a_ref,
        (role_ref[...], pick(got_q_ref[...], got_p_ref[...])),
        (pick(own_q, own_p), pick(got_q, got_p)),
    )
    write_block(
        b_ref,
        (pick(got_p_ref[...], got_q_ref[...]), other_ref[...]),
        (pick(got_p, got_q), pick(own_p, own_q)),
    )


def row_numbers(plan, slab, blk, role, rows, turns, place):
    chip = slab >> 1
    number = place
    for i, turn in enumerate(turns):
        for other in (0, 1):
            core = role ^ other
            p_shard = blk * (2 * plan.chip_count) + 2 * peer(chip, turn, plan.chip_count) + core
            q_shard = (2 * chip + core) * plan.blk_count + peer(blk, turn, plan.blk_count)
            p_base = p_shard * rows if turn < plan.chip_count else -(1 << 24)
            q_base = q_shard * rows if turn < plan.blk_count else -(1 << 25)
            start = (2 * i + other) * rows
            base = jnp.where(role == 0, p_base, q_base) - start
            number = jnp.where(place >= start, place + base, number)
    return number


def gradient(plan, rows, scalars, a_turns, a_refs, a_norm, b_turns, b_refs):
    slab, blk = (ref[0] for ref in scalars)
    a, b = read_rows(a_refs, rows), read_rows(b_refs, rows)
    scale = 2.0 / math.sqrt(a.shape[1])
    scores = scale * lax.dot_general(
        a, b, (((1,), (1,)), ((), ())), preferred_element_type=jnp.float32
    )
    role = slab & 1
    numbers = functools.partial(row_numbers, plan, slab, blk, rows=rows)
    a_place = lax.broadcasted_iota(jnp.int32, (a.shape[0], 1), 0)
    b_place = lax.broadcasted_iota(jnp.int32, (1, b.shape[0]), 1)
    a_number = numbers(role, turns=a_turns, place=a_place)
    b_number = numbers(1 - role, turns=b_turns, place=b_place)
    weights = (0.5 * scale) * (
        jnp.exp(scores - a_norm)
        + jnp.exp(scores - norm_row(b_refs, rows))
        - 2.0 * (a_number == b_number).astype(jnp.float32)
    )
    high = weights.astype(jnp.bfloat16)
    low = (weights - high.astype(jnp.float32)).astype(jnp.bfloat16)
    if b.shape[0] >= 256:
        both = jnp.dot(jnp.concatenate([high, low], axis=0), b, preferred_element_type=jnp.float32)
        return both[: a.shape[0]] + both[a.shape[0] :]
    return jnp.dot(
        jnp.concatenate([high, low], axis=1),
        jnp.concatenate([b, b], axis=0),
        preferred_element_type=jnp.float32,
    )


def early_kernel(plan, rows, a_turns, b_turns, *refs):
    scalars, refs, (out_ref, norm_ref) = refs[:2], refs[3:-2], refs[-2:]
    a_refs, b_refs = refs[: len(a_turns)], refs[len(a_turns) :]
    a_norm = norm_column(a_refs, rows)
    out_ref[...] = gradient(plan, rows, scalars, a_turns, a_refs, a_norm, b_turns, b_refs)
    norm_ref[...] = jnp.broadcast_to(a_norm, norm_ref.shape)


def late_kernel(plan, rows, a_turns, b_turns, *refs):
    scalars, (early_ref, norm_ref), refs = refs[:2], refs[2:4], refs[4:]
    n = len(a_turns)
    a_refs, b_refs, out_refs = refs[:n], refs[n : n + len(b_turns)], refs[n + len(b_turns) :]
    total = early_ref[...] + gradient(
        plan, rows, scalars, a_turns, a_refs, norm_ref[:, 0:1], b_turns, b_refs
    )
    write_partial(out_refs[0], total[:rows])
    write_partial(out_refs[1], total[rows : 2 * rows])
    for i, out_ref in enumerate(out_refs[2:], 1):
        write_partial(out_ref, total[2 * rows * i : 2 * rows * (i + 1)], 2)


def own_kernel(plan, rows, turns, *refs):
    scalars, a_refs, b_refs, out_ref = refs[:2], refs[2:3], refs[3:-1], refs[-1]
    a_norm = norm_column(a_refs, rows)
    out_ref[...] = gradient(plan, rows, scalars, turns[:1], a_refs, a_norm, turns, b_refs)


def tiles(block):
    rows, width = block.shape
    return [
        block[:, i : i + LANES].reshape(rows // SIZE_ROWS, SIZE_ROWS, LANES)
        for i in range(0, width, LANES)
    ]


def write_partial(ref, block, parts=1):
    size = block.shape[0] // parts
    chunks = tiles(block)
    largest = functools.reduce(
        jnp.maximum, [jnp.max(jnp.abs(chunk), axis=0, keepdims=True) for chunk in chunks]
    )
    power = jnp.ceil(jnp.log2(jnp.maximum(largest, 1e-30))) - 10.0
    factor = jnp.exp2(-power)
    for i, chunk in enumerate(chunks):
        chunk = (chunk * factor).reshape(block.shape[0], LANES)
        for j in range(parts):
            start = (j * len(chunks) + i) * size
            ref[start : start + size] = chunk[j * size : (j + 1) * size]
    start = len(chunks) * block.shape[0]
    copies = (ref.shape[0] - start) // SIZE_ROWS
    ref[start:] = jnp.concatenate([power[0]] * copies, axis=0)


def spread_kernel(value_ref, out_ref):
    out_ref[...] = jnp.full(out_ref.shape, value_ref[0], jnp.float32)


def read_partials(refs, rows, start):
    factors = [jnp.exp2(ref[ref.shape[0] - SIZE_ROWS :])[None] for ref in refs]
    chunks = (refs[0].shape[0] - SIZE_ROWS - start) // rows
    for i in range(chunks):
        yield sum(
            ref[start + i * rows : start + (i + 1) * rows].reshape(-1, SIZE_ROWS, LANES) * factor
            for ref, factor in zip(refs, factors)
        )


def sum_kernel(own_ref, *refs):
    partial_refs, (keep_ref, give_ref) = refs[:-2], refs[-2:]
    rows, width = own_ref.shape
    half = rows // 2
    chunks = width // LANES
    own = tiles(own_ref[...])
    gives = []
    first = [0.0] * chunks
    second = [0.0] * chunks
    if partial_refs:
        both = list(read_partials(partial_refs, half, 0))
        first, second = both[:chunks], both[chunks:]
    for i, total in enumerate(own):
        n = half // SIZE_ROWS
        keep_ref[:, i * LANES : (i + 1) * LANES] = (total[:n] + first[i]).reshape(half, LANES)
        gives.append((total[n:] + second[i]).reshape(half, LANES))
    write_partial(give_ref, jnp.concatenate(gives, axis=1))


def end_kernel(loss_ref, keep_ref, here_ref, got_ref, there_ref, *refs):
    last_refs, (keep_out, got_out) = refs[:-2], refs[-2:]
    rows, width = keep_ref.shape
    loss = loss_ref[...][None]
    here = read_partials([here_ref], rows, 0)
    keeps = read_partials([last_refs[0]], rows, 0)
    gots = read_partials([got_ref, there_ref, last_refs[1]], rows, 0)
    for i, (keep, a, b, got) in enumerate(zip(tiles(keep_ref[...]), here, keeps, gots)):
        lanes = slice(i * LANES, (i + 1) * LANES)
        keep_out[:, lanes] = ((keep + a + b) * loss).reshape(rows, LANES)
        got_out[:, lanes] = (got * loss).reshape(rows, LANES)


VMEM = pl.BlockSpec(memory_space=pltpu.VMEM)
SMEM = pl.BlockSpec(memory_space=pltpu.SMEM)


def call(kernel, name, scalars, arrays, out_shape, mebibytes, flops=0):
    return pl.pallas_call(
        kernel,
        out_shape=out_shape,
        in_specs=[SMEM] * len(scalars) + [VMEM] * len(arrays),
        out_specs=[VMEM] * len(out_shape),
        name=name,
        compiler_params=pltpu.CompilerParams(vmem_limit_bytes=mebibytes * 1024 * 1024),
        cost_estimate=pl.CostEstimate(flops=flops, bytes_accessed=0, transcendentals=0),
    )(*(x.reshape(1) for x in scalars), *arrays)


def local(plan, queries, passages, query_lognorm, passage_lognorm, loss_cotangent):
    rows, width = queries.shape
    count = plan.group_size
    chunk_rows = 2 * rows * (width // LANES)
    slab = lax.axis_index("slab")
    blk = lax.axis_index("blk")
    core = slab & 1

    def swapped(block):
        return lax.ppermute(block, AXES, plan.core_pairs())

    packed = jax.ShapeDtypeStruct((chunk_rows + NORM_ROWS, LANES), jnp.bfloat16)
    mine, others = call(
        pack_kernel,
        "pack",
        (slab,),
        (
            jnp.where(core == 1, queries, passages),
            jnp.where(core == 1, passages, queries),
            swapped(queries),
            swapped(passages),
            jnp.concatenate([query_lognorm, passage_lognorm]).reshape(1, -1),
            swapped(query_lognorm).reshape(1, -1),
        ),
        [packed, packed],
        4,
    )

    (loss,) = call(
        spread_kernel,
        "spread",
        (loss_cotangent,),
        (),
        [jax.ShapeDtypeStruct((SIZE_ROWS, LANES), jnp.float32)],
        1,
        flops=10**9,
    )

    a_parts, b_parts = [mine], [others]
    for turn in range(1, count):
        back = [(to, at) for at, to in plan.group_pairs(turn)]
        a_parts.append(lax.ppermute(mine, AXES, back))
        b_parts.append(swapped(a_parts[-1]))

    scalars = (slab, blk)
    turns = list(range(count))
    last = turns[1:3]
    soon = [i for i in turns if i not in last]
    a_others = a_parts[1:]
    other_rows = 2 * rows * (count - 1)
    early = call(
        functools.partial(early_kernel, plan, rows, turns[1:], soon),
        "early",
        scalars,
        (loss, *a_others, *(b_parts[i] for i in soon)),
        [
            jax.ShapeDtypeStruct((other_rows, width), jnp.float32),
            jax.ShapeDtypeStruct((other_rows, LANES), jnp.float32),
        ],
        3 * count,
        flops=10**9,
    )
    partials = call(
        functools.partial(late_kernel, plan, rows, turns[1:], last),
        "late",
        scalars,
        (*early, *a_others, *(b_parts[i] for i in last)),
        [
            jax.ShapeDtypeStruct((chunk_rows // 2 + n * SIZE_ROWS, LANES), jnp.float32)
            for n in (1, 3)
        ]
        + [jax.ShapeDtypeStruct((chunk_rows + SIZE_ROWS, LANES), jnp.float32)] * (count - 2),
        3 * count,
    )
    (own,) = call(
        functools.partial(own_kernel, plan, rows, turns),
        "own",
        scalars,
        (mine, *b_parts),
        [jax.ShapeDtypeStruct((2 * rows, width), jnp.float32)],
        3 * count,
        flops=10**9,
    )
    half = jax.ShapeDtypeStruct((rows, width), jnp.float32)

    def crossed(partial, turn, across=False):
        return lax.ppermute(partial.astype(jnp.float16), AXES, plan.group_pairs(turn, across))

    def wide(block):
        return block.astype(jnp.float32)

    arrived = [crossed(x, turn) for turn, x in enumerate(partials[2:], 2)]
    last = [wide(crossed(partials[0], 1)), wide(crossed(partials[1], 1, True))]
    piece = jax.ShapeDtypeStruct((chunk_rows // 2 + SIZE_ROWS, LANES), jnp.float32)
    keep, give = call(
        sum_kernel, "sum", (), (own, *(wide(x) for x in arrived[1:])), [half, piece], 2 * count
    )
    got = wide(swapped(give.astype(jnp.float16)))
    there = wide(swapped(arrived[0][chunk_rows // 2 :]))
    keep, got = call(
        end_kernel, "end", (), (loss, keep, wide(arrived[0]), got, there, *last), [half, half], 4
    )
    return jnp.where(core == 1, keep, got), jnp.where(core == 1, got, keep)


def solution(mesh):
    plan = Plan(mesh.shape["slab"], mesh.shape["blk"])
    return jax.shard_map(
        functools.partial(local, plan),
        mesh=mesh,
        in_specs=(
            P(("slab", "blk"), None),
            P(("blk", "slab"), None),
            P(("slab", "blk")),
            P("blk"),
            P(),
        ),
        out_specs=(P(("slab", "blk"), None), P(("blk", "slab"), None)),
        check_vma=False,
    )
```

```python
import functools
import math

import jax
import jax.numpy as jnp
from jax import lax
from jax.experimental import pallas as pl
from jax.experimental.pallas import tpu as pltpu
from jax.sharding import PartitionSpec as P

AXES = ("slab", "blk")
LANES = 128
NORM_ROWS = 16
SIZE_ROWS = 8


def peer(index, step, count):
    if count & (count - 1) == 0:
        return index ^ step
    return (index + step) % count


class Plan:
    def __init__(self, slab_count, blk_count):
        self.blk_count = blk_count
        self.chip_count = slab_count // 2
        self.group_size = max(self.chip_count, blk_count)

    def device(self, chip, core, blk):
        return (2 * chip + core) * self.blk_count + blk

    def each(self):
        for chip in range(self.chip_count):
            for blk in range(self.blk_count):
                yield chip, blk

    def core_pairs(self):
        return [
            (self.device(chip, core, blk), self.device(chip, 1 - core, blk))
            for chip, blk in self.each()
            for core in (0, 1)
        ]

    def group_pairs(self, turn, across=False):
        pairs = []
        for chip, blk in self.each():
            if turn < self.chip_count:
                other = peer(chip, turn, self.chip_count)
                pairs.append((self.device(chip, 0, blk), self.device(other, int(across), blk)))
            if turn < self.blk_count:
                other = peer(blk, turn, self.blk_count)
                pairs.append((self.device(chip, 1, blk), self.device(chip, 1 - across, other)))
        return pairs


def column(values, first, rows):
    shape = (rows, values.shape[1])
    lane = lax.broadcasted_iota(jnp.int32, shape, 1)
    row = lax.broadcasted_iota(jnp.int32, shape, 0)
    picked = jnp.where(lane == row + first, jnp.broadcast_to(values, shape), 0.0)
    return jnp.sum(picked, axis=1, keepdims=True)


def as_row(values, lanes):
    shape = (values.shape[0], lanes)
    lane = lax.broadcasted_iota(jnp.int32, shape, 1)
    row = lax.broadcasted_iota(jnp.int32, shape, 0)
    picked = jnp.where(lane == row, jnp.broadcast_to(values, shape), 0.0)
    return jnp.sum(picked, axis=0, keepdims=True)


def split_three(values):
    high = values.astype(jnp.bfloat16).astype(jnp.float32)
    middle = (values - high).astype(jnp.bfloat16).astype(jnp.float32)
    return high, middle, values - high - middle


def write_block(out_ref, halves, norms):
    rows, width = halves[0].shape
    for chunk in range(width // LANES):
        for half in (0, 1):
            start = (2 * chunk + half) * rows
            out_ref[start : start + rows] = halves[half][:, chunk * LANES : (chunk + 1) * LANES]
    shape = (NORM_ROWS, LANES)
    row = lax.broadcasted_iota(jnp.int32, shape, 0)
    tail = jnp.zeros(shape, jnp.float32)
    for half in (0, 1):
        for i, part in enumerate(split_three(as_row(norms[half], LANES))):
            tail = jnp.where(row == 3 * half + i, jnp.broadcast_to(part, shape), tail)
    out_ref[2 * rows * (width // LANES) :] = tail.astype(jnp.bfloat16)


def read_rows(refs, rows):
    size = 2 * rows
    chunks = (refs[0].shape[0] - NORM_ROWS) // size
    parts = [[ref[size * i : size * (i + 1)] for i in range(chunks)] for ref in refs]
    return jnp.concatenate([jnp.concatenate(part, axis=1) for part in parts], axis=0)


def read_norms(refs):
    norms = []
    for ref in refs:
        tail = ref[ref.shape[0] - NORM_ROWS :].astype(jnp.float32)
        norms += [tail[i : i + 1] + tail[i + 1 : i + 2] + tail[i + 2 : i + 3] for i in (0, 3)]
    return norms


def norm_column(refs, rows):
    return jnp.concatenate([column(norm, 0, rows) for norm in read_norms(refs)], axis=0)


def norm_row(refs, rows):
    norms, per_row = read_norms(refs), LANES // rows
    lane = lax.broadcasted_iota(jnp.int32, (1, LANES), 1)
    pieces = []
    for start in range(0, len(norms), per_row):
        piece = norms[start]
        for i, norm in enumerate(norms[start + 1 : start + per_row], 1):
            piece = jnp.where(lane >= i * rows, pltpu.roll(norm, i * rows, 1), piece)
        pieces.append(piece)
    return jnp.concatenate(pieces, axis=1)[:, : len(norms) * rows]


def pack_kernel(
    slab_ref, role_ref, other_ref, got_q_ref, got_p_ref, norm_ref, got_norm_ref, a_ref, b_ref
):
    rows = role_ref.shape[0]
    slab = slab_ref[0]
    pick = functools.partial(jnp.where, (slab & 1) == 1)
    own_q = column(norm_ref[...], 0, rows)
    got_q = column(got_norm_ref[...], 0, rows)
    own_p = column(norm_ref[...], (1 + slab) * rows, rows)
    got_p = column(norm_ref[...], (1 + (slab ^ 1)) * rows, rows)
    write_block(
        a_ref,
        (role_ref[...], pick(got_q_ref[...], got_p_ref[...])),
        (pick(own_q, own_p), pick(got_q, got_p)),
    )
    write_block(
        b_ref,
        (pick(got_p_ref[...], got_q_ref[...]), other_ref[...]),
        (pick(got_p, got_q), pick(own_p, own_q)),
    )


def row_numbers(plan, slab, blk, role, rows, turns, place):
    chip = slab >> 1
    number = place
    for i, turn in enumerate(turns):
        for other in (0, 1):
            core = role ^ other
            p_shard = blk * (2 * plan.chip_count) + 2 * peer(chip, turn, plan.chip_count) + core
            q_shard = (2 * chip + core) * plan.blk_count + peer(blk, turn, plan.blk_count)
            p_base = p_shard * rows if turn < plan.chip_count else -(1 << 24)
            q_base = q_shard * rows if turn < plan.blk_count else -(1 << 25)
            start = (2 * i + other) * rows
            base = jnp.where(role == 0, p_base, q_base) - start
            number = jnp.where(place >= start, place + base, number)
    return number


def gradient(plan, rows, scalars, a_turns, a_refs, a_norm, b_turns, b_refs):
    slab, blk = (ref[0] for ref in scalars)
    a, b = read_rows(a_refs, rows), read_rows(b_refs, rows)
    scale = 2.0 / math.sqrt(a.shape[1])
    scores = scale * lax.dot_general(
        a, b, (((1,), (1,)), ((), ())), preferred_element_type=jnp.float32
    )
    role = slab & 1
    numbers = functools.partial(row_numbers, plan, slab, blk, rows=rows)
    a_place = lax.broadcasted_iota(jnp.int32, (a.shape[0], 1), 0)
    b_place = lax.broadcasted_iota(jnp.int32, (1, b.shape[0]), 1)
    a_number = numbers(role, turns=a_turns, place=a_place)
    b_number = numbers(1 - role, turns=b_turns, place=b_place)
    weights = (0.5 * scale) * (
        jnp.exp(scores - a_norm)
        + jnp.exp(scores - norm_row(b_refs, rows))
        - 2.0 * (a_number == b_number).astype(jnp.float32)
    )
    high = weights.astype(jnp.bfloat16)
    low = (weights - high.astype(jnp.float32)).astype(jnp.bfloat16)
    if b.shape[0] >= 256:
        both = jnp.dot(jnp.concatenate([high, low], axis=0), b, preferred_element_type=jnp.float32)
        return both[: a.shape[0]] + both[a.shape[0] :]
    return jnp.dot(
        jnp.concatenate([high, low], axis=1),
        jnp.concatenate([b, b], axis=0),
        preferred_element_type=jnp.float32,
    )


def early_kernel(plan, rows, a_turns, b_turns, *refs):
    scalars, refs, (out_ref, norm_ref) = refs[:2], refs[3:-2], refs[-2:]
    a_refs, b_refs = refs[: len(a_turns)], refs[len(a_turns) :]
    a_norm = norm_column(a_refs, rows)
    out_ref[...] = gradient(plan, rows, scalars, a_turns, a_refs, a_norm, b_turns, b_refs)
    norm_ref[...] = jnp.broadcast_to(a_norm, norm_ref.shape)


def late_kernel(plan, rows, a_turns, b_turns, *refs):
    scalars, (early_ref, norm_ref), refs = refs[:2], refs[2:4], refs[4:]
    n = len(a_turns)
    a_refs, b_refs, out_refs = refs[:n], refs[n : n + len(b_turns)], refs[n + len(b_turns) :]
    total = early_ref[...] + gradient(
        plan, rows, scalars, a_turns, a_refs, norm_ref[:, 0:1], b_turns, b_refs
    )
    write_partial(out_refs[0], total[:rows])
    write_partial(out_refs[1], total[rows : 2 * rows])
    for i, out_ref in enumerate(out_refs[2:], 1):
        write_partial(out_ref, total[2 * rows * i : 2 * rows * (i + 1)], 2)


def own_kernel(plan, rows, turns, *refs):
    scalars, a_refs, b_refs, out_ref = refs[:2], refs[2:3], refs[3:-1], refs[-1]
    a_norm = norm_column(a_refs, rows)
    out_ref[...] = gradient(plan, rows, scalars, turns[:1], a_refs, a_norm, turns, b_refs)


def tiles(block):
    rows, width = block.shape
    return [
        block[:, i : i + LANES].reshape(rows // SIZE_ROWS, SIZE_ROWS, LANES)
        for i in range(0, width, LANES)
    ]


def write_partial(ref, block, parts=1):
    size = block.shape[0] // parts
    chunks = tiles(block)
    largest = functools.reduce(
        jnp.maximum, [jnp.max(jnp.abs(chunk), axis=0, keepdims=True) for chunk in chunks]
    )
    power = jnp.ceil(jnp.log2(jnp.maximum(largest, 1e-30))) - 10.0
    factor = jnp.exp2(-power)
    for i, chunk in enumerate(chunks):
        chunk = (chunk * factor).reshape(block.shape[0], LANES)
        for j in range(parts):
            start = (j * len(chunks) + i) * size
            ref[start : start + size] = chunk[j * size : (j + 1) * size]
    start = len(chunks) * block.shape[0]
    copies = (ref.shape[0] - start) // SIZE_ROWS
    ref[start:] = jnp.concatenate([power[0]] * copies, axis=0)


def spread_kernel(value_ref, out_ref):
    out_ref[...] = jnp.full(out_ref.shape, value_ref[0], jnp.float32)


def read_partials(refs, rows, start):
    factors = [jnp.exp2(ref[ref.shape[0] - SIZE_ROWS :])[None] for ref in refs]
    chunks = (refs[0].shape[0] - SIZE_ROWS - start) // rows
    for i in range(chunks):
        yield sum(
            ref[start + i * rows : start + (i + 1) * rows].reshape(-1, SIZE_ROWS, LANES) * factor
            for ref, factor in zip(refs, factors)
        )


def sum_kernel(own_ref, *refs):
    partial_refs, (keep_ref, give_ref) = refs[:-2], refs[-2:]
    rows, width = own_ref.shape
    half = rows // 2
    chunks = width // LANES
    own = tiles(own_ref[...])
    gives = []
    first = [0.0] * chunks
    second = [0.0] * chunks
    if partial_refs:
        both = list(read_partials(partial_refs, half, 0))
        first, second = both[:chunks], both[chunks:]
    for i, total in enumerate(own):
        n = half // SIZE_ROWS
        keep_ref[:, i * LANES : (i + 1) * LANES] = (total[:n] + first[i]).reshape(half, LANES)
        gives.append((total[n:] + second[i]).reshape(half, LANES))
    write_partial(give_ref, jnp.concatenate(gives, axis=1))


def end_kernel(loss_ref, keep_ref, here_ref, got_ref, there_ref, *refs):
    last_refs, (keep_out, got_out) = refs[:-2], refs[-2:]
    rows, width = keep_ref.shape
    loss = loss_ref[...][None]
    here = read_partials([here_ref], rows, 0)
    keeps = read_partials([last_refs[0]], rows, 0)
    gots = read_partials([got_ref, there_ref, last_refs[1]], rows, 0)
    for i, (keep, a, b, got) in enumerate(zip(tiles(keep_ref[...]), here, keeps, gots)):
        lanes = slice(i * LANES, (i + 1) * LANES)
        keep_out[:, lanes] = ((keep + a + b) * loss).reshape(rows, LANES)
        got_out[:, lanes] = (got * loss).reshape(rows, LANES)


VMEM = pl.BlockSpec(memory_space=pltpu.VMEM)
SMEM = pl.BlockSpec(memory_space=pltpu.SMEM)


def call(kernel, name, scalars, arrays, out_shape, mebibytes, flops=0):
    return pl.pallas_call(
        kernel,
        out_shape=out_shape,
        in_specs=[SMEM] * len(scalars) + [VMEM] * len(arrays),
        out_specs=[VMEM] * len(out_shape),
        name=name,
        compiler_params=pltpu.CompilerParams(vmem_limit_bytes=mebibytes * 1024 * 1024),
        cost_estimate=pl.CostEstimate(flops=flops, bytes_accessed=0, transcendentals=0),
    )(*(x.reshape(1) for x in scalars), *arrays)


def local(plan, queries, passages, query_lognorm, passage_lognorm, loss_cotangent):
    rows, width = queries.shape
    count = plan.group_size
    chunk_rows = 2 * rows * (width // LANES)
    slab = lax.axis_index("slab")
    blk = lax.axis_index("blk")
    core = slab & 1

    def swapped(block):
        return lax.ppermute(block, AXES, plan.core_pairs())

    packed = jax.ShapeDtypeStruct((chunk_rows + NORM_ROWS, LANES), jnp.bfloat16)
    mine, others = call(
        pack_kernel,
        "pack",
        (slab,),
        (
            jnp.where(core == 1, queries, passages),
            jnp.where(core == 1, passages, queries),
            swapped(queries),
            swapped(passages),
            jnp.concatenate([query_lognorm, passage_lognorm]).reshape(1, -1),
            swapped(query_lognorm).reshape(1, -1),
        ),
        [packed, packed],
        4,
    )

    (loss,) = call(
        spread_kernel,
        "spread",
        (loss_cotangent,),
        (),
        [jax.ShapeDtypeStruct((SIZE_ROWS, LANES), jnp.float32)],
        1,
        flops=10**9,
    )

    a_parts, b_parts = [mine], [others]
    for turn in range(1, count):
        back = [(to, at) for at, to in plan.group_pairs(turn)]
        a_parts.append(lax.ppermute(mine, AXES, back))
        b_parts.append(swapped(a_parts[-1]))

    scalars = (slab, blk)
    turns = list(range(count))
    last = turns[1:3]
    soon = [i for i in turns if i not in last]
    a_others = a_parts[1:]
    other_rows = 2 * rows * (count - 1)
    early = call(
        functools.partial(early_kernel, plan, rows, turns[1:], soon),
        "early",
        scalars,
        (loss, *a_others, *(b_parts[i] for i in soon)),
        [
            jax.ShapeDtypeStruct((other_rows, width), jnp.float32),
            jax.ShapeDtypeStruct((other_rows, LANES), jnp.float32),
        ],
        3 * count,
        flops=10**9,
    )
    partials = call(
        functools.partial(late_kernel, plan, rows, turns[1:], last),
        "late",
        scalars,
        (*early, *a_others, *(b_parts[i] for i in last)),
        [
            jax.ShapeDtypeStruct((chunk_rows // 2 + n * SIZE_ROWS, LANES), jnp.float32)
            for n in (3, 5)
        ]
        + [jax.ShapeDtypeStruct((chunk_rows + SIZE_ROWS, LANES), jnp.float32)] * (count - 2),
        3 * count,
    )
    (own,) = call(
        functools.partial(own_kernel, plan, rows, turns),
        "own",
        scalars,
        (mine, *b_parts),
        [jax.ShapeDtypeStruct((2 * rows, width), jnp.float32)],
        3 * count,
        flops=10**9,
    )
    half = jax.ShapeDtypeStruct((rows, width), jnp.float32)

    def crossed(partial, turn, across=False):
        return lax.ppermute(partial.astype(jnp.float16), AXES, plan.group_pairs(turn, across))

    def wide(block):
        return block.astype(jnp.float32)

    arrived = [crossed(x, turn) for turn, x in enumerate(partials[2:], 2)]
    last = [wide(crossed(partials[0], 1)), wide(crossed(partials[1], 1, True))]
    piece = jax.ShapeDtypeStruct((chunk_rows // 2 + 2 * SIZE_ROWS, LANES), jnp.float32)
    keep, give = call(
        sum_kernel, "sum", (), (own, *(wide(x) for x in arrived[:-1])), [half, piece], 2 * count
    )
    got = wide(swapped(give.astype(jnp.float16)))
    there = wide(swapped(arrived[-1][chunk_rows // 2 :]))
    keep, got = call(
        end_kernel, "end", (), (loss, keep, wide(arrived[-1]), got, there, *last), [half, half], 4
    )
    return jnp.where(core == 1, keep, got), jnp.where(core == 1, got, keep)


def solution(mesh):
    plan = Plan(mesh.shape["slab"], mesh.shape["blk"])
    return jax.shard_map(
        functools.partial(local, plan),
        mesh=mesh,
        in_specs=(
            P(("slab", "blk"), None),
            P(("blk", "slab"), None),
            P(("slab", "blk")),
            P("blk"),
            P(),
        ),
        out_specs=(P(("slab", "blk"), None), P(("blk", "slab"), None)),
        check_vma=False,
    )
```

```python
import functools
import math

import jax
import jax.numpy as jnp
from jax import lax
from jax.experimental import pallas as pl
from jax.experimental.pallas import tpu as pltpu
from jax.sharding import PartitionSpec as P

AXES = ("slab", "blk")
LANES = 128
NORM_ROWS = 16
SIZE_ROWS = 8


def peer(index, step, count):
    if count & (count - 1) == 0:
        return index ^ step
    return (index + step) % count


class Plan:
    def __init__(self, slab_count, blk_count):
        self.blk_count = blk_count
        self.chip_count = slab_count // 2
        self.group_size = max(self.chip_count, blk_count)

    def device(self, chip, core, blk):
        return (2 * chip + core) * self.blk_count + blk

    def each(self):
        for chip in range(self.chip_count):
            for blk in range(self.blk_count):
                yield chip, blk

    def core_pairs(self):
        return [
            (self.device(chip, core, blk), self.device(chip, 1 - core, blk))
            for chip, blk in self.each()
            for core in (0, 1)
        ]

    def group_pairs(self, turn, across=False):
        pairs = []
        for chip, blk in self.each():
            if turn < self.chip_count:
                other = peer(chip, turn, self.chip_count)
                pairs.append((self.device(chip, 0, blk), self.device(other, int(across), blk)))
            if turn < self.blk_count:
                other = peer(blk, turn, self.blk_count)
                pairs.append((self.device(chip, 1, blk), self.device(chip, 1 - across, other)))
        return pairs


def column(values, first, rows):
    shape = (rows, values.shape[1])
    lane = lax.broadcasted_iota(jnp.int32, shape, 1)
    row = lax.broadcasted_iota(jnp.int32, shape, 0)
    picked = jnp.where(lane == row + first, jnp.broadcast_to(values, shape), 0.0)
    return jnp.sum(picked, axis=1, keepdims=True)


def as_row(values, lanes):
    shape = (values.shape[0], lanes)
    lane = lax.broadcasted_iota(jnp.int32, shape, 1)
    row = lax.broadcasted_iota(jnp.int32, shape, 0)
    picked = jnp.where(lane == row, jnp.broadcast_to(values, shape), 0.0)
    return jnp.sum(picked, axis=0, keepdims=True)


def split_three(values):
    high = values.astype(jnp.bfloat16).astype(jnp.float32)
    middle = (values - high).astype(jnp.bfloat16).astype(jnp.float32)
    return high, middle, values - high - middle


def write_block(out_ref, halves, norms):
    rows, width = halves[0].shape
    for chunk in range(width // LANES):
        for half in (0, 1):
            start = (2 * chunk + half) * rows
            out_ref[start : start + rows] = halves[half][:, chunk * LANES : (chunk + 1) * LANES]
    shape = (NORM_ROWS, LANES)
    row = lax.broadcasted_iota(jnp.int32, shape, 0)
    tail = jnp.zeros(shape, jnp.float32)
    for half in (0, 1):
        for i, part in enumerate(split_three(as_row(norms[half], LANES))):
            tail = jnp.where(row == 3 * half + i, jnp.broadcast_to(part, shape), tail)
    out_ref[2 * rows * (width // LANES) :] = tail.astype(jnp.bfloat16)


def read_rows(refs, rows):
    size = 2 * rows
    chunks = (refs[0].shape[0] - NORM_ROWS) // size
    parts = [[ref[size * i : size * (i + 1)] for i in range(chunks)] for ref in refs]
    return jnp.concatenate([jnp.concatenate(part, axis=1) for part in parts], axis=0)


def read_norms(refs):
    norms = []
    for ref in refs:
        tail = ref[ref.shape[0] - NORM_ROWS :].astype(jnp.float32)
        norms += [tail[i : i + 1] + tail[i + 1 : i + 2] + tail[i + 2 : i + 3] for i in (0, 3)]
    return norms


def norm_column(refs, rows):
    return jnp.concatenate([column(norm, 0, rows) for norm in read_norms(refs)], axis=0)


def norm_row(refs, rows):
    norms, per_row = read_norms(refs), LANES // rows
    lane = lax.broadcasted_iota(jnp.int32, (1, LANES), 1)
    pieces = []
    for start in range(0, len(norms), per_row):
        piece = norms[start]
        for i, norm in enumerate(norms[start + 1 : start + per_row], 1):
            piece = jnp.where(lane >= i * rows, pltpu.roll(norm, i * rows, 1), piece)
        pieces.append(piece)
    return jnp.concatenate(pieces, axis=1)[:, : len(norms) * rows]


def mark_kernel(slab_ref, out_ref):
    out_ref[...] = jnp.full(out_ref.shape, slab_ref[0], jnp.int32)


def pack_kernel(
    slab_ref, _, q_ref, p_ref, norm_ref, got_q_ref, got_p_ref, got_norm_ref, a_ref, b_ref
):
    rows = q_ref.shape[0]
    slab = slab_ref[0]
    pick = functools.partial(jnp.where, (slab & 1) == 1)
    own_q = column(norm_ref[...], 0, rows)
    got_q = column(got_norm_ref[...], 0, rows)
    own_p = column(norm_ref[...], (1 + slab) * rows, rows)
    got_p = column(norm_ref[...], (1 + (slab ^ 1)) * rows, rows)
    write_block(
        a_ref,
        (pick(q_ref[...], p_ref[...]), pick(got_q_ref[...], got_p_ref[...])),
        (pick(own_q, own_p), pick(got_q, got_p)),
    )
    write_block(
        b_ref,
        (pick(got_p_ref[...], got_q_ref[...]), pick(p_ref[...], q_ref[...])),
        (pick(got_p, got_q), pick(own_p, own_q)),
    )


def row_numbers(plan, slab, blk, role, rows, turns, place):
    chip = slab >> 1
    number = place
    for i, turn in enumerate(turns):
        for other in (0, 1):
            core = role ^ other
            p_shard = blk * (2 * plan.chip_count) + 2 * peer(chip, turn, plan.chip_count) + core
            q_shard = (2 * chip + core) * plan.blk_count + peer(blk, turn, plan.blk_count)
            p_base = p_shard * rows if turn < plan.chip_count else -(1 << 24)
            q_base = q_shard * rows if turn < plan.blk_count else -(1 << 25)
            start = (2 * i + other) * rows
            base = jnp.where(role == 0, p_base, q_base) - start
            number = jnp.where(place >= start, place + base, number)
    return number


def gradient(plan, rows, scalars, a_turns, a_refs, a_norm, b_turns, b_refs):
    slab, blk = (ref[0] for ref in scalars)
    a, b = read_rows(a_refs, rows), read_rows(b_refs, rows)
    scale = 2.0 / math.sqrt(a.shape[1])
    scores = scale * lax.dot_general(
        a, b, (((1,), (1,)), ((), ())), preferred_element_type=jnp.float32
    )
    role = slab & 1
    numbers = functools.partial(row_numbers, plan, slab, blk, rows=rows)
    a_place = lax.broadcasted_iota(jnp.int32, (a.shape[0], 1), 0)
    b_place = lax.broadcasted_iota(jnp.int32, (1, b.shape[0]), 1)
    a_number = numbers(role, turns=a_turns, place=a_place)
    b_number = numbers(1 - role, turns=b_turns, place=b_place)
    weights = (0.5 * scale) * (
        jnp.exp(scores - a_norm)
        + jnp.exp(scores - norm_row(b_refs, rows))
        - 2.0 * (a_number == b_number).astype(jnp.float32)
    )
    high = weights.astype(jnp.bfloat16)
    low = (weights - high.astype(jnp.float32)).astype(jnp.bfloat16)
    if b.shape[0] >= 256:
        both = jnp.dot(jnp.concatenate([high, low], axis=0), b, preferred_element_type=jnp.float32)
        return both[: a.shape[0]] + both[a.shape[0] :]
    return jnp.dot(
        jnp.concatenate([high, low], axis=1),
        jnp.concatenate([b, b], axis=0),
        preferred_element_type=jnp.float32,
    )


def early_kernel(plan, rows, a_turns, b_turns, *refs):
    scalars, refs, (out_ref, norm_ref) = refs[:2], refs[3:-2], refs[-2:]
    a_refs, b_refs = refs[: len(a_turns)], refs[len(a_turns) :]
    a_norm = norm_column(a_refs, rows)
    out_ref[...] = gradient(plan, rows, scalars, a_turns, a_refs, a_norm, b_turns, b_refs)
    norm_ref[...] = jnp.broadcast_to(a_norm, norm_ref.shape)


def late_kernel(plan, rows, a_turns, b_turns, *refs):
    scalars, (early_ref, norm_ref), refs = refs[:2], refs[2:4], refs[4:]
    n = len(a_turns)
    a_refs, b_refs, out_refs = refs[:n], refs[n : n + len(b_turns)], refs[n + len(b_turns) :]
    total = early_ref[...] + gradient(
        plan, rows, scalars, a_turns, a_refs, norm_ref[:, 0:1], b_turns, b_refs
    )
    write_partial(out_refs[0], total[:rows])
    write_partial(out_refs[1], total[rows : 2 * rows])
    for i, out_ref in enumerate(out_refs[2:], 1):
        write_partial(out_ref, total[2 * rows * i : 2 * rows * (i + 1)], 2)


def own_kernel(plan, rows, turns, *refs):
    scalars, a_refs, b_refs, out_ref = refs[:2], refs[2:3], refs[3:-1], refs[-1]
    a_norm = norm_column(a_refs, rows)
    out_ref[...] = gradient(plan, rows, scalars, turns[:1], a_refs, a_norm, turns, b_refs)


def tiles(block):
    rows, width = block.shape
    return [
        block[:, i : i + LANES].reshape(rows // SIZE_ROWS, SIZE_ROWS, LANES)
        for i in range(0, width, LANES)
    ]


def write_partial(ref, block, parts=1):
    size = block.shape[0] // parts
    chunks = tiles(block)
    largest = functools.reduce(
        jnp.maximum, [jnp.max(jnp.abs(chunk), axis=0, keepdims=True) for chunk in chunks]
    )
    power = jnp.ceil(jnp.log2(jnp.maximum(largest, 1e-30))) - 10.0
    factor = jnp.exp2(-power)
    for i, chunk in enumerate(chunks):
        chunk = (chunk * factor).reshape(block.shape[0], LANES)
        for j in range(parts):
            start = (j * len(chunks) + i) * size
            ref[start : start + size] = chunk[j * size : (j + 1) * size]
    start = len(chunks) * block.shape[0]
    copies = (ref.shape[0] - start) // SIZE_ROWS
    ref[start:] = jnp.concatenate([power[0]] * copies, axis=0)


def spread_kernel(value_ref, out_ref):
    out_ref[...] = jnp.full(out_ref.shape, value_ref[0], jnp.float32)


def read_partials(refs, rows, start):
    factors = [jnp.exp2(ref[ref.shape[0] - SIZE_ROWS :])[None] for ref in refs]
    chunks = (refs[0].shape[0] - SIZE_ROWS - start) // rows
    for i in range(chunks):
        yield sum(
            ref[start + i * rows : start + (i + 1) * rows].reshape(-1, SIZE_ROWS, LANES) * factor
            for ref, factor in zip(refs, factors)
        )


def sum_kernel(own_ref, *refs):
    partial_refs, (keep_ref, give_ref) = refs[:-2], refs[-2:]
    rows, width = own_ref.shape
    half = rows // 2
    chunks = width // LANES
    own = tiles(own_ref[...])
    gives = []
    first = [0.0] * chunks
    second = [0.0] * chunks
    if partial_refs:
        both = list(read_partials(partial_refs, half, 0))
        first, second = both[:chunks], both[chunks:]
    for i, total in enumerate(own):
        n = half // SIZE_ROWS
        keep_ref[:, i * LANES : (i + 1) * LANES] = (total[:n] + first[i]).reshape(half, LANES)
        gives.append((total[n:] + second[i]).reshape(half, LANES))
    write_partial(give_ref, jnp.concatenate(gives, axis=1))


def end_kernel(loss_ref, keep_ref, here_ref, got_ref, there_ref, *refs):
    last_refs, (keep_out, got_out) = refs[:-2], refs[-2:]
    rows, width = keep_ref.shape
    loss = loss_ref[...][None]
    here = read_partials([here_ref], rows, 0)
    keeps = read_partials([last_refs[0]], rows, 0)
    gots = read_partials([got_ref, there_ref, last_refs[1]], rows, 0)
    for i, (keep, a, b, got) in enumerate(zip(tiles(keep_ref[...]), here, keeps, gots)):
        lanes = slice(i * LANES, (i + 1) * LANES)
        keep_out[:, lanes] = ((keep + a + b) * loss).reshape(rows, LANES)
        got_out[:, lanes] = (got * loss).reshape(rows, LANES)


VMEM = pl.BlockSpec(memory_space=pltpu.VMEM)
SMEM = pl.BlockSpec(memory_space=pltpu.SMEM)


def call(kernel, name, scalars, arrays, out_shape, mebibytes, flops=0):
    return pl.pallas_call(
        kernel,
        out_shape=out_shape,
        in_specs=[SMEM] * len(scalars) + [VMEM] * len(arrays),
        out_specs=[VMEM] * len(out_shape),
        name=name,
        compiler_params=pltpu.CompilerParams(vmem_limit_bytes=mebibytes * 1024 * 1024),
        cost_estimate=pl.CostEstimate(flops=flops, bytes_accessed=0, transcendentals=0),
    )(*(x.reshape(1) for x in scalars), *arrays)


def local(plan, queries, passages, query_lognorm, passage_lognorm, loss_cotangent):
    rows, width = queries.shape
    count = plan.group_size
    chunk_rows = 2 * rows * (width // LANES)
    slab = lax.axis_index("slab")
    blk = lax.axis_index("blk")
    core = slab & 1

    def swapped(block):
        return lax.ppermute(block, AXES, plan.core_pairs())

    packed = jax.ShapeDtypeStruct((chunk_rows + NORM_ROWS, LANES), jnp.bfloat16)
    (mark,) = call(
        mark_kernel, "mark", (slab,), (), [jax.ShapeDtypeStruct((8, LANES), jnp.int32)], 1, flops=4*10**9
    )
    mine, others = call(
        pack_kernel,
        "pack",
        (slab,),
        (
            mark,
            queries,
            passages,
            jnp.concatenate([query_lognorm, passage_lognorm]).reshape(1, -1),
            swapped(queries),
            swapped(passages),
            swapped(query_lognorm).reshape(1, -1),
        ),
        [packed, packed],
        4,
    )

    (loss,) = call(
        spread_kernel,
        "spread",
        (loss_cotangent,),
        (),
        [jax.ShapeDtypeStruct((SIZE_ROWS, LANES), jnp.float32)],
        1,
        flops=10**9,
    )

    a_parts, b_parts = [mine], [others]
    for turn in range(1, count):
        back = [(to, at) for at, to in plan.group_pairs(turn)]
        a_parts.append(lax.ppermute(mine, AXES, back))
        b_parts.append(swapped(a_parts[-1]))

    scalars = (slab, blk)
    turns = list(range(count))
    last = turns[1:3]
    soon = [i for i in turns if i not in last]
    a_others = a_parts[1:]
    other_rows = 2 * rows * (count - 1)
    early = call(
        functools.partial(early_kernel, plan, rows, turns[1:], soon),
        "early",
        scalars,
        (loss, *a_others, *(b_parts[i] for i in soon)),
        [
            jax.ShapeDtypeStruct((other_rows, width), jnp.float32),
            jax.ShapeDtypeStruct((other_rows, LANES), jnp.float32),
        ],
        3 * count,
        flops=10**9,
    )
    partials = call(
        functools.partial(late_kernel, plan, rows, turns[1:], last),
        "late",
        scalars,
        (*early, *a_others, *(b_parts[i] for i in last)),
        [
            jax.ShapeDtypeStruct((chunk_rows // 2 + n * SIZE_ROWS, LANES), jnp.float32)
            for n in (3, 5)
        ]
        + [jax.ShapeDtypeStruct((chunk_rows + SIZE_ROWS, LANES), jnp.float32)] * (count - 2),
        3 * count,
    )
    (own,) = call(
        functools.partial(own_kernel, plan, rows, turns),
        "own",
        scalars,
        (mine, *b_parts),
        [jax.ShapeDtypeStruct((2 * rows, width), jnp.float32)],
        3 * count,
        flops=10**9,
    )
    half = jax.ShapeDtypeStruct((rows, width), jnp.float32)

    def crossed(partial, turn, across=False):
        return lax.ppermute(partial.astype(jnp.float16), AXES, plan.group_pairs(turn, across))

    def wide(block):
        return block.astype(jnp.float32)

    arrived = [crossed(x, turn) for turn, x in enumerate(partials[2:], 2)]
    last = [wide(crossed(partials[0], 1)), wide(crossed(partials[1], 1, True))]
    piece = jax.ShapeDtypeStruct((chunk_rows // 2 + 2 * SIZE_ROWS, LANES), jnp.float32)
    keep, give = call(
        sum_kernel, "sum", (), (own, *(wide(x) for x in arrived[:-1])), [half, piece], 2 * count
    )
    got = wide(swapped(give.astype(jnp.float16)))
    there = wide(swapped(arrived[-1][chunk_rows // 2 :]))
    keep, got = call(
        end_kernel, "end", (), (loss, keep, wide(arrived[-1]), got, there, *last), [half, half], 4
    )
    return jnp.where(core == 1, keep, got), jnp.where(core == 1, got, keep)


def solution(mesh):
    plan = Plan(mesh.shape["slab"], mesh.shape["blk"])
    return jax.shard_map(
        functools.partial(local, plan),
        mesh=mesh,
        in_specs=(
            P(("slab", "blk"), None),
            P(("blk", "slab"), None),
            P(("slab", "blk")),
            P("blk"),
            P(),
        ),
        out_specs=(P(("slab", "blk"), None), P(("blk", "slab"), None)),
        check_vma=False,
    )
```

```python
import functools
import math

import jax
import jax.numpy as jnp
from jax import lax
from jax.experimental import pallas as pl
from jax.experimental.pallas import tpu as pltpu
from jax.sharding import PartitionSpec as P

AXES = ("slab", "blk")
LANES = 128
NORM_ROWS = 16
SIZE_ROWS = 8


def peer(index, step, count):
    if count & (count - 1) == 0:
        return index ^ step
    return (index + step) % count


class Plan:
    def __init__(self, slab_count, blk_count):
        self.blk_count = blk_count
        self.chip_count = slab_count // 2
        self.group_size = max(self.chip_count, blk_count)

    def device(self, chip, core, blk):
        return (2 * chip + core) * self.blk_count + blk

    def each(self):
        for chip in range(self.chip_count):
            for blk in range(self.blk_count):
                yield chip, blk

    def core_pairs(self):
        return [
            (self.device(chip, core, blk), self.device(chip, 1 - core, blk))
            for chip, blk in self.each()
            for core in (0, 1)
        ]

    def group_pairs(self, turn, across=False):
        pairs = []
        for chip, blk in self.each():
            if turn < self.chip_count:
                other = peer(chip, turn, self.chip_count)
                pairs.append((self.device(chip, 0, blk), self.device(other, int(across), blk)))
            if turn < self.blk_count:
                other = peer(blk, turn, self.blk_count)
                pairs.append((self.device(chip, 1, blk), self.device(chip, 1 - across, other)))
        return pairs


def column(values, first, rows):
    shape = (rows, values.shape[1])
    lane = lax.broadcasted_iota(jnp.int32, shape, 1)
    row = lax.broadcasted_iota(jnp.int32, shape, 0)
    picked = jnp.where(lane == row + first, jnp.broadcast_to(values, shape), 0.0)
    return jnp.sum(picked, axis=1, keepdims=True)


def as_row(values, lanes):
    shape = (values.shape[0], lanes)
    lane = lax.broadcasted_iota(jnp.int32, shape, 1)
    row = lax.broadcasted_iota(jnp.int32, shape, 0)
    picked = jnp.where(lane == row, jnp.broadcast_to(values, shape), 0.0)
    return jnp.sum(picked, axis=0, keepdims=True)


def split_three(values):
    high = values.astype(jnp.bfloat16).astype(jnp.float32)
    middle = (values - high).astype(jnp.bfloat16).astype(jnp.float32)
    return high, middle, values - high - middle


def write_block(out_ref, halves, norms):
    rows, width = halves[0].shape
    for chunk in range(width // LANES):
        for half in (0, 1):
            start = (2 * chunk + half) * rows
            out_ref[start : start + rows] = halves[half][:, chunk * LANES : (chunk + 1) * LANES]
    shape = (NORM_ROWS, LANES)
    row = lax.broadcasted_iota(jnp.int32, shape, 0)
    tail = jnp.zeros(shape, jnp.float32)
    for half in (0, 1):
        for i, part in enumerate(split_three(as_row(norms[half], LANES))):
            tail = jnp.where(row == 3 * half + i, jnp.broadcast_to(part, shape), tail)
    out_ref[2 * rows * (width // LANES) :] = tail.astype(jnp.bfloat16)


def read_rows(refs, rows):
    size = 2 * rows
    chunks = (refs[0].shape[0] - NORM_ROWS) // size
    parts = [[ref[size * i : size * (i + 1)] for i in range(chunks)] for ref in refs]
    return jnp.concatenate([jnp.concatenate(part, axis=1) for part in parts], axis=0)


def read_norms(refs):
    norms = []
    for ref in refs:
        tail = ref[ref.shape[0] - NORM_ROWS :].astype(jnp.float32)
        norms += [tail[i : i + 1] + tail[i + 1 : i + 2] + tail[i + 2 : i + 3] for i in (0, 3)]
    return norms


def norm_column(refs, rows):
    return jnp.concatenate([column(norm, 0, rows) for norm in read_norms(refs)], axis=0)


def norm_row(refs, rows):
    norms, per_row = read_norms(refs), LANES // rows
    lane = lax.broadcasted_iota(jnp.int32, (1, LANES), 1)
    pieces = []
    for start in range(0, len(norms), per_row):
        piece = norms[start]
        for i, norm in enumerate(norms[start + 1 : start + per_row], 1):
            piece = jnp.where(lane >= i * rows, pltpu.roll(norm, i * rows, 1), piece)
        pieces.append(piece)
    return jnp.concatenate(pieces, axis=1)[:, : len(norms) * rows]


def mark_kernel(slab_ref, out_ref):
    out_ref[...] = jnp.full(out_ref.shape, slab_ref[0], jnp.int32)


def pack_kernel(
    other, slab_ref, _, q_ref, p_ref, norm_ref, got_q_ref, got_p_ref, got_norm_ref, out_ref
):
    rows = q_ref.shape[0]
    slab = slab_ref[0]
    pick = functools.partial(jnp.where, (slab & 1) == 1)
    own_q = column(norm_ref[...], 0, rows)
    got_q = column(got_norm_ref[...], 0, rows)
    own_p = column(norm_ref[...], (1 + slab) * rows, rows)
    got_p = column(norm_ref[...], (1 + (slab ^ 1)) * rows, rows)
    if other:
        write_block(
            out_ref,
            (pick(got_p_ref[...], got_q_ref[...]), pick(p_ref[...], q_ref[...])),
            (pick(got_p, got_q), pick(own_p, own_q)),
        )
    else:
        write_block(
            out_ref,
            (pick(q_ref[...], p_ref[...]), pick(got_q_ref[...], got_p_ref[...])),
            (pick(own_q, own_p), pick(got_q, got_p)),
        )


def row_numbers(plan, slab, blk, role, rows, turns, place):
    chip = slab >> 1
    number = place
    for i, turn in enumerate(turns):
        for other in (0, 1):
            core = role ^ other
            p_shard = blk * (2 * plan.chip_count) + 2 * peer(chip, turn, plan.chip_count) + core
            q_shard = (2 * chip + core) * plan.blk_count + peer(blk, turn, plan.blk_count)
            p_base = p_shard * rows if turn < plan.chip_count else -(1 << 24)
            q_base = q_shard * rows if turn < plan.blk_count else -(1 << 25)
            start = (2 * i + other) * rows
            base = jnp.where(role == 0, p_base, q_base) - start
            number = jnp.where(place >= start, place + base, number)
    return number


def gradient(plan, rows, scalars, a_turns, a_refs, a_norm, b_turns, b_refs):
    slab, blk = (ref[0] for ref in scalars)
    a, b = read_rows(a_refs, rows), read_rows(b_refs, rows)
    scale = 2.0 / math.sqrt(a.shape[1])
    scores = scale * lax.dot_general(
        a, b, (((1,), (1,)), ((), ())), preferred_element_type=jnp.float32
    )
    role = slab & 1
    numbers = functools.partial(row_numbers, plan, slab, blk, rows=rows)
    a_place = lax.broadcasted_iota(jnp.int32, (a.shape[0], 1), 0)
    b_place = lax.broadcasted_iota(jnp.int32, (1, b.shape[0]), 1)
    a_number = numbers(role, turns=a_turns, place=a_place)
    b_number = numbers(1 - role, turns=b_turns, place=b_place)
    weights = (0.5 * scale) * (
        jnp.exp(scores - a_norm)
        + jnp.exp(scores - norm_row(b_refs, rows))
        - 2.0 * (a_number == b_number).astype(jnp.float32)
    )
    high = weights.astype(jnp.bfloat16)
    low = (weights - high.astype(jnp.float32)).astype(jnp.bfloat16)
    if b.shape[0] >= 256:
        both = jnp.dot(jnp.concatenate([high, low], axis=0), b, preferred_element_type=jnp.float32)
        return both[: a.shape[0]] + both[a.shape[0] :]
    return jnp.dot(
        jnp.concatenate([high, low], axis=1),
        jnp.concatenate([b, b], axis=0),
        preferred_element_type=jnp.float32,
    )


def early_kernel(plan, rows, a_turns, b_turns, *refs):
    scalars, refs, (out_ref, norm_ref) = refs[:2], refs[3:-2], refs[-2:]
    a_refs, b_refs = refs[: len(a_turns)], refs[len(a_turns) :]
    a_norm = norm_column(a_refs, rows)
    out_ref[...] = gradient(plan, rows, scalars, a_turns, a_refs, a_norm, b_turns, b_refs)
    norm_ref[...] = jnp.broadcast_to(a_norm, norm_ref.shape)


def late_kernel(plan, rows, a_turns, b_turns, *refs):
    scalars, (early_ref, norm_ref), refs = refs[:2], refs[2:4], refs[4:]
    n = len(a_turns)
    a_refs, b_refs, out_refs = refs[:n], refs[n : n + len(b_turns)], refs[n + len(b_turns) :]
    total = early_ref[...] + gradient(
        plan, rows, scalars, a_turns, a_refs, norm_ref[:, 0:1], b_turns, b_refs
    )
    write_partial(out_refs[0], total[:rows])
    write_partial(out_refs[1], total[rows : 2 * rows])
    for i, out_ref in enumerate(out_refs[2:], 1):
        write_partial(out_ref, total[2 * rows * i : 2 * rows * (i + 1)], 2)


def own_kernel(plan, rows, turns, *refs):
    scalars, a_refs, b_refs, out_ref = refs[:2], refs[2:3], refs[3:-1], refs[-1]
    a_norm = norm_column(a_refs, rows)
    out_ref[...] = gradient(plan, rows, scalars, turns[:1], a_refs, a_norm, turns, b_refs)


def tiles(block):
    rows, width = block.shape
    return [
        block[:, i : i + LANES].reshape(rows // SIZE_ROWS, SIZE_ROWS, LANES)
        for i in range(0, width, LANES)
    ]


def write_partial(ref, block, parts=1):
    size = block.shape[0] // parts
    chunks = tiles(block)
    largest = functools.reduce(
        jnp.maximum, [jnp.max(jnp.abs(chunk), axis=0, keepdims=True) for chunk in chunks]
    )
    power = jnp.ceil(jnp.log2(jnp.maximum(largest, 1e-30))) - 10.0
    factor = jnp.exp2(-power)
    for i, chunk in enumerate(chunks):
        chunk = (chunk * factor).reshape(block.shape[0], LANES)
        for j in range(parts):
            start = (j * len(chunks) + i) * size
            ref[start : start + size] = chunk[j * size : (j + 1) * size]
    start = len(chunks) * block.shape[0]
    copies = (ref.shape[0] - start) // SIZE_ROWS
    ref[start:] = jnp.concatenate([power[0]] * copies, axis=0)


def spread_kernel(value_ref, out_ref):
    out_ref[...] = jnp.full(out_ref.shape, value_ref[0], jnp.float32)


def read_partials(refs, rows, start):
    factors = [jnp.exp2(ref[ref.shape[0] - SIZE_ROWS :])[None] for ref in refs]
    chunks = (refs[0].shape[0] - SIZE_ROWS - start) // rows
    for i in range(chunks):
        yield sum(
            ref[start + i * rows : start + (i + 1) * rows].reshape(-1, SIZE_ROWS, LANES) * factor
            for ref, factor in zip(refs, factors)
        )


def sum_kernel(own_ref, *refs):
    partial_refs, (keep_ref, give_ref) = refs[:-2], refs[-2:]
    rows, width = own_ref.shape
    half = rows // 2
    chunks = width // LANES
    own = tiles(own_ref[...])
    gives = []
    first = [0.0] * chunks
    second = [0.0] * chunks
    if partial_refs:
        both = list(read_partials(partial_refs, half, 0))
        first, second = both[:chunks], both[chunks:]
    for i, total in enumerate(own):
        n = half // SIZE_ROWS
        keep_ref[:, i * LANES : (i + 1) * LANES] = (total[:n] + first[i]).reshape(half, LANES)
        gives.append((total[n:] + second[i]).reshape(half, LANES))
    write_partial(give_ref, jnp.concatenate(gives, axis=1))


def end_kernel(loss_ref, keep_ref, here_ref, got_ref, there_ref, *refs):
    last_refs, (keep_out, got_out) = refs[:-2], refs[-2:]
    rows, width = keep_ref.shape
    loss = loss_ref[...][None]
    here = read_partials([here_ref], rows, 0)
    keeps = read_partials([last_refs[0]], rows, 0)
    gots = read_partials([got_ref, there_ref, last_refs[1]], rows, 0)
    for i, (keep, a, b, got) in enumerate(zip(tiles(keep_ref[...]), here, keeps, gots)):
        lanes = slice(i * LANES, (i + 1) * LANES)
        keep_out[:, lanes] = ((keep + a + b) * loss).reshape(rows, LANES)
        got_out[:, lanes] = (got * loss).reshape(rows, LANES)


VMEM = pl.BlockSpec(memory_space=pltpu.VMEM)
SMEM = pl.BlockSpec(memory_space=pltpu.SMEM)


def call(kernel, name, scalars, arrays, out_shape, mebibytes, flops=0):
    return pl.pallas_call(
        kernel,
        out_shape=out_shape,
        in_specs=[SMEM] * len(scalars) + [VMEM] * len(arrays),
        out_specs=[VMEM] * len(out_shape),
        name=name,
        compiler_params=pltpu.CompilerParams(vmem_limit_bytes=mebibytes * 1024 * 1024),
        cost_estimate=pl.CostEstimate(flops=flops, bytes_accessed=0, transcendentals=0),
    )(*(x.reshape(1) for x in scalars), *arrays)


def local(plan, queries, passages, query_lognorm, passage_lognorm, loss_cotangent):
    rows, width = queries.shape
    count = plan.group_size
    chunk_rows = 2 * rows * (width // LANES)
    slab = lax.axis_index("slab")
    blk = lax.axis_index("blk")
    core = slab & 1

    def swapped(block):
        return lax.ppermute(block, AXES, plan.core_pairs())

    packed = jax.ShapeDtypeStruct((chunk_rows + NORM_ROWS, LANES), jnp.bfloat16)
    (mark,) = call(
        mark_kernel, "mark", (slab,), (), [jax.ShapeDtypeStruct((8, LANES), jnp.int32)], 1, flops=4*10**9
    )
    arrays = (
        mark,
        queries,
        passages,
        jnp.concatenate([query_lognorm, passage_lognorm]).reshape(1, -1),
        swapped(queries),
        swapped(passages),
        swapped(query_lognorm).reshape(1, -1),
    )
    (mine,), (others,) = (
        call(functools.partial(pack_kernel, other), "pack", (slab,), arrays, [packed], 4)
        for other in (False, True)
    )
    (loss,) = call(
        spread_kernel,
        "spread",
        (loss_cotangent,),
        (),
        [jax.ShapeDtypeStruct((SIZE_ROWS, LANES), jnp.float32)],
        1,
        flops=10**9,
    )

    a_parts, b_parts = [mine], [others]
    for turn in range(1, count):
        back = [(to, at) for at, to in plan.group_pairs(turn)]
        a_parts.append(lax.ppermute(mine, AXES, back))
        b_parts.append(swapped(a_parts[-1]))

    scalars = (slab, blk)
    turns = list(range(count))
    last = turns[1:3]
    soon = [i for i in turns if i not in last]
    a_others = a_parts[1:]
    other_rows = 2 * rows * (count - 1)
    early = call(
        functools.partial(early_kernel, plan, rows, turns[1:], soon),
        "early",
        scalars,
        (loss, *a_others, *(b_parts[i] for i in soon)),
        [
            jax.ShapeDtypeStruct((other_rows, width), jnp.float32),
            jax.ShapeDtypeStruct((other_rows, LANES), jnp.float32),
        ],
        3 * count,
        flops=10**9,
    )
    partials = call(
        functools.partial(late_kernel, plan, rows, turns[1:], last),
        "late",
        scalars,
        (*early, *a_others, *(b_parts[i] for i in last)),
        [
            jax.ShapeDtypeStruct((chunk_rows // 2 + n * SIZE_ROWS, LANES), jnp.float32)
            for n in (3, 5)
        ]
        + [jax.ShapeDtypeStruct((chunk_rows + SIZE_ROWS, LANES), jnp.float32)] * (count - 2),
        3 * count,
    )
    (own,) = call(
        functools.partial(own_kernel, plan, rows, turns),
        "own",
        scalars,
        (mine, *b_parts),
        [jax.ShapeDtypeStruct((2 * rows, width), jnp.float32)],
        3 * count,
        flops=10**9,
    )
    half = jax.ShapeDtypeStruct((rows, width), jnp.float32)

    def crossed(partial, turn, across=False):
        return lax.ppermute(partial.astype(jnp.float16), AXES, plan.group_pairs(turn, across))

    def wide(block):
        return block.astype(jnp.float32)

    arrived = [crossed(x, turn) for turn, x in enumerate(partials[2:], 2)]
    last = [wide(crossed(partials[0], 1)), wide(crossed(partials[1], 1, True))]
    piece = jax.ShapeDtypeStruct((chunk_rows // 2 + 2 * SIZE_ROWS, LANES), jnp.float32)
    keep, give = call(
        sum_kernel, "sum", (), (own, *(wide(x) for x in arrived[:-1])), [half, piece], 2 * count
    )
    got = wide(swapped(give.astype(jnp.float16)))
    there = wide(swapped(arrived[-1][chunk_rows // 2 :]))
    keep, got = call(
        end_kernel, "end", (), (loss, keep, wide(arrived[-1]), got, there, *last), [half, half], 4
    )
    return jnp.where(core == 1, keep, got), jnp.where(core == 1, got, keep)


def solution(mesh):
    plan = Plan(mesh.shape["slab"], mesh.shape["blk"])
    return jax.shard_map(
        functools.partial(local, plan),
        mesh=mesh,
        in_specs=(
            P(("slab", "blk"), None),
            P(("blk", "slab"), None),
            P(("slab", "blk")),
            P("blk"),
            P(),
        ),
        out_specs=(P(("slab", "blk"), None), P(("blk", "slab"), None)),
        check_vma=False,
    )
```

```python
import functools
import math

import jax
import jax.numpy as jnp
from jax import lax
from jax.experimental import pallas as pl
from jax.experimental.pallas import tpu as pltpu
from jax.sharding import PartitionSpec as P

AXES = ("slab", "blk")
LANES = 128
NORM_ROWS = 16
SIZE_ROWS = 8


def peer(index, step, count):
    if count & (count - 1) == 0:
        return index ^ step
    return (index + step) % count


class Plan:
    def __init__(self, slab_count, blk_count):
        self.blk_count = blk_count
        self.chip_count = slab_count // 2
        self.group_size = max(self.chip_count, blk_count)

    def device(self, chip, core, blk):
        return (2 * chip + core) * self.blk_count + blk

    def each(self):
        for chip in range(self.chip_count):
            for blk in range(self.blk_count):
                yield chip, blk

    def core_pairs(self):
        return [
            (self.device(chip, core, blk), self.device(chip, 1 - core, blk))
            for chip, blk in self.each()
            for core in (0, 1)
        ]

    def group_pairs(self, turn, across=False):
        pairs = []
        for chip, blk in self.each():
            if turn < self.chip_count:
                other = peer(chip, turn, self.chip_count)
                pairs.append((self.device(chip, 0, blk), self.device(other, int(across), blk)))
            if turn < self.blk_count:
                other = peer(blk, turn, self.blk_count)
                pairs.append((self.device(chip, 1, blk), self.device(chip, 1 - across, other)))
        return pairs


def column(values, first, rows):
    shape = (rows, values.shape[1])
    lane = lax.broadcasted_iota(jnp.int32, shape, 1)
    row = lax.broadcasted_iota(jnp.int32, shape, 0)
    picked = jnp.where(lane == row + first, jnp.broadcast_to(values, shape), 0.0)
    return jnp.sum(picked, axis=1, keepdims=True)


def as_row(values, lanes):
    shape = (values.shape[0], lanes)
    lane = lax.broadcasted_iota(jnp.int32, shape, 1)
    row = lax.broadcasted_iota(jnp.int32, shape, 0)
    picked = jnp.where(lane == row, jnp.broadcast_to(values, shape), 0.0)
    return jnp.sum(picked, axis=0, keepdims=True)


def split_three(values):
    high = values.astype(jnp.bfloat16).astype(jnp.float32)
    middle = (values - high).astype(jnp.bfloat16).astype(jnp.float32)
    return high, middle, values - high - middle


def write_block(out_ref, halves, norms):
    rows, width = halves[0].shape
    for chunk in range(width // LANES):
        for half in (0, 1):
            start = (2 * chunk + half) * rows
            out_ref[start : start + rows] = halves[half][:, chunk * LANES : (chunk + 1) * LANES]
    shape = (NORM_ROWS, LANES)
    row = lax.broadcasted_iota(jnp.int32, shape, 0)
    tail = jnp.zeros(shape, jnp.float32)
    for half in (0, 1):
        for i, part in enumerate(split_three(as_row(norms[half], LANES))):
            tail = jnp.where(row == 3 * half + i, jnp.broadcast_to(part, shape), tail)
    out_ref[2 * rows * (width // LANES) :] = tail.astype(jnp.bfloat16)


def read_rows(refs, rows):
    size = 2 * rows
    chunks = (refs[0].shape[0] - NORM_ROWS) // size
    parts = [[ref[size * i : size * (i + 1)] for i in range(chunks)] for ref in refs]
    return jnp.concatenate([jnp.concatenate(part, axis=1) for part in parts], axis=0)


def read_norms(refs):
    norms = []
    for ref in refs:
        tail = ref[ref.shape[0] - NORM_ROWS :].astype(jnp.float32)
        norms += [tail[i : i + 1] + tail[i + 1 : i + 2] + tail[i + 2 : i + 3] for i in (0, 3)]
    return norms


def norm_column(refs, rows):
    return jnp.concatenate([column(norm, 0, rows) for norm in read_norms(refs)], axis=0)


def norm_row(refs, rows):
    norms, per_row = read_norms(refs), LANES // rows
    lane = lax.broadcasted_iota(jnp.int32, (1, LANES), 1)
    pieces = []
    for start in range(0, len(norms), per_row):
        piece = norms[start]
        for i, norm in enumerate(norms[start + 1 : start + per_row], 1):
            piece = jnp.where(lane >= i * rows, pltpu.roll(norm, i * rows, 1), piece)
        pieces.append(piece)
    return jnp.concatenate(pieces, axis=1)[:, : len(norms) * rows]


def mark_kernel(slab_ref, out_ref):
    out_ref[...] = jnp.full(out_ref.shape, slab_ref[0], jnp.int32)


def pack_kernel(
    slab_ref, _, q_ref, p_ref, norm_ref, got_q_ref, got_p_ref, got_norm_ref, a_ref, b_ref
):
    rows = q_ref.shape[0]
    slab = slab_ref[0]
    pick = functools.partial(jnp.where, (slab & 1) == 1)
    own_q = column(norm_ref[...], 0, rows)
    got_q = column(got_norm_ref[...], 0, rows)
    own_p = column(norm_ref[...], (1 + slab) * rows, rows)
    got_p = column(norm_ref[...], (1 + (slab ^ 1)) * rows, rows)
    write_block(
        a_ref,
        (pick(q_ref[...], p_ref[...]), pick(got_q_ref[...], got_p_ref[...])),
        (pick(own_q, own_p), pick(got_q, got_p)),
    )
    write_block(
        b_ref,
        (pick(got_p_ref[...], got_q_ref[...]), pick(p_ref[...], q_ref[...])),
        (pick(got_p, got_q), pick(own_p, own_q)),
    )


def row_numbers(plan, slab, blk, role, rows, turns, place):
    chip = slab >> 1
    number = place
    for i, turn in enumerate(turns):
        for other in (0, 1):
            core = role ^ other
            p_shard = blk * (2 * plan.chip_count) + 2 * peer(chip, turn, plan.chip_count) + core
            q_shard = (2 * chip + core) * plan.blk_count + peer(blk, turn, plan.blk_count)
            p_base = p_shard * rows if turn < plan.chip_count else -(1 << 24)
            q_base = q_shard * rows if turn < plan.blk_count else -(1 << 25)
            start = (2 * i + other) * rows
            base = jnp.where(role == 0, p_base, q_base) - start
            number = jnp.where(place >= start, place + base, number)
    return number


def gradient(plan, rows, scalars, a_turns, a_refs, a_norm, b_turns, b_refs):
    slab, blk = (ref[0] for ref in scalars)
    a, b = read_rows(a_refs, rows), read_rows(b_refs, rows)
    scale = 2.0 / math.sqrt(a.shape[1])
    scores = scale * lax.dot_general(
        a, b, (((1,), (1,)), ((), ())), preferred_element_type=jnp.float32
    )
    role = slab & 1
    numbers = functools.partial(row_numbers, plan, slab, blk, rows=rows)
    a_place = lax.broadcasted_iota(jnp.int32, (a.shape[0], 1), 0)
    b_place = lax.broadcasted_iota(jnp.int32, (1, b.shape[0]), 1)
    a_number = numbers(role, turns=a_turns, place=a_place)
    b_number = numbers(1 - role, turns=b_turns, place=b_place)
    weights = (0.5 * scale) * (
        jnp.exp(scores - a_norm)
        + jnp.exp(scores - norm_row(b_refs, rows))
        - 2.0 * (a_number == b_number).astype(jnp.float32)
    )
    high = weights.astype(jnp.bfloat16)
    low = (weights - high.astype(jnp.float32)).astype(jnp.bfloat16)
    if b.shape[0] >= 256:
        both = jnp.dot(jnp.concatenate([high, low], axis=0), b, preferred_element_type=jnp.float32)
        return both[: a.shape[0]] + both[a.shape[0] :]
    return jnp.dot(
        jnp.concatenate([high, low], axis=1),
        jnp.concatenate([b, b], axis=0),
        preferred_element_type=jnp.float32,
    )


def early_kernel(plan, rows, a_turns, b_turns, *refs):
    scalars, refs, (out_ref, norm_ref) = refs[:2], refs[3:-2], refs[-2:]
    a_refs, b_refs = refs[: len(a_turns)], refs[len(a_turns) :]
    a_norm = norm_column(a_refs, rows)
    out_ref[...] = gradient(plan, rows, scalars, a_turns, a_refs, a_norm, b_turns, b_refs)
    norm_ref[...] = jnp.broadcast_to(a_norm, norm_ref.shape)


def late_kernel(plan, rows, a_turns, b_turns, *refs):
    scalars, (early_ref, norm_ref), refs = refs[:2], refs[2:4], refs[4:]
    n = len(a_turns)
    a_refs, b_refs, out_refs = refs[:n], refs[n : n + len(b_turns)], refs[n + len(b_turns) :]
    total = early_ref[...] + gradient(
        plan, rows, scalars, a_turns, a_refs, norm_ref[:, 0:1], b_turns, b_refs
    )
    write_partial(out_refs[0], total[:rows])
    write_partial(out_refs[1], total[rows : 2 * rows])
    for i, out_ref in enumerate(out_refs[2:], 1):
        write_partial(out_ref, total[2 * rows * i : 2 * rows * (i + 1)], 2)


def own_kernel(plan, rows, turns, *refs):
    scalars, a_refs, b_refs, out_ref = refs[:2], refs[2:3], refs[3:-1], refs[-1]
    a_norm = norm_column(a_refs, rows)
    out_ref[...] = gradient(plan, rows, scalars, turns[:1], a_refs, a_norm, turns, b_refs)


def tiles(block):
    rows, width = block.shape
    return [
        block[:, i : i + LANES].reshape(rows // SIZE_ROWS, SIZE_ROWS, LANES)
        for i in range(0, width, LANES)
    ]


def write_partial(ref, block, parts=1):
    size = block.shape[0] // parts
    chunks = tiles(block)
    largest = functools.reduce(
        jnp.maximum, [jnp.max(jnp.abs(chunk), axis=0, keepdims=True) for chunk in chunks]
    )
    power = jnp.ceil(jnp.log2(jnp.maximum(largest, 1e-30))) - 10.0
    factor = jnp.exp2(-power)
    for i, chunk in enumerate(chunks):
        chunk = (chunk * factor).reshape(block.shape[0], LANES)
        for j in range(parts):
            start = (j * len(chunks) + i) * size
            ref[start : start + size] = chunk[j * size : (j + 1) * size]
    start = len(chunks) * block.shape[0]
    copies = (ref.shape[0] - start) // SIZE_ROWS
    ref[start:] = jnp.concatenate([power[0]] * copies, axis=0)


def spread_kernel(value_ref, out_ref):
    out_ref[...] = jnp.full(out_ref.shape, value_ref[0], jnp.float32)


def read_partials(refs, rows, start):
    factors = [jnp.exp2(ref[ref.shape[0] - SIZE_ROWS :])[None] for ref in refs]
    chunks = (refs[0].shape[0] - SIZE_ROWS - start) // rows
    for i in range(chunks):
        yield sum(
            ref[start + i * rows : start + (i + 1) * rows].reshape(-1, SIZE_ROWS, LANES) * factor
            for ref, factor in zip(refs, factors)
        )


def sum_kernel(own_ref, *refs):
    partial_refs, (keep_ref, give_ref) = refs[:-2], refs[-2:]
    rows, width = own_ref.shape
    half = rows // 2
    chunks = width // LANES
    own = tiles(own_ref[...])
    gives = []
    first = [0.0] * chunks
    second = [0.0] * chunks
    if partial_refs:
        both = list(read_partials(partial_refs, half, 0))
        first, second = both[:chunks], both[chunks:]
    for i, total in enumerate(own):
        n = half // SIZE_ROWS
        keep_ref[:, i * LANES : (i + 1) * LANES] = (total[:n] + first[i]).reshape(half, LANES)
        gives.append((total[n:] + second[i]).reshape(half, LANES))
    write_partial(give_ref, jnp.concatenate(gives, axis=1))


def end_kernel(slab_ref, loss_ref, keep_ref, here_ref, got_ref, there_ref, *refs):
    last_refs, (q_out, p_out) = refs[:-2], refs[-2:]
    pick = functools.partial(jnp.where, (slab_ref[0] & 1) == 1)
    rows, width = keep_ref.shape
    loss = loss_ref[...][None]
    here = read_partials([here_ref], rows, 0)
    keeps = read_partials([last_refs[0]], rows, 0)
    gots = read_partials([got_ref, there_ref, last_refs[1]], rows, 0)
    for i, (keep, a, b, got) in enumerate(zip(tiles(keep_ref[...]), here, keeps, gots)):
        lanes = slice(i * LANES, (i + 1) * LANES)
        keep, got = (((x * loss).reshape(rows, LANES)) for x in (keep + a + b, got))
        q_out[:, lanes], p_out[:, lanes] = pick(keep, got), pick(got, keep)


VMEM = pl.BlockSpec(memory_space=pltpu.VMEM)
SMEM = pl.BlockSpec(memory_space=pltpu.SMEM)


def call(kernel, name, scalars, arrays, out_shape, mebibytes, flops=0):
    return pl.pallas_call(
        kernel,
        out_shape=out_shape,
        in_specs=[SMEM] * len(scalars) + [VMEM] * len(arrays),
        out_specs=[VMEM] * len(out_shape),
        name=name,
        compiler_params=pltpu.CompilerParams(vmem_limit_bytes=mebibytes * 1024 * 1024),
        cost_estimate=pl.CostEstimate(flops=flops, bytes_accessed=0, transcendentals=0),
    )(*(x.reshape(1) for x in scalars), *arrays)


def local(plan, queries, passages, query_lognorm, passage_lognorm, loss_cotangent):
    rows, width = queries.shape
    count = plan.group_size
    chunk_rows = 2 * rows * (width // LANES)
    slab = lax.axis_index("slab")
    blk = lax.axis_index("blk")
    core = slab & 1

    def swapped(block):
        return lax.ppermute(block, AXES, plan.core_pairs())

    packed = jax.ShapeDtypeStruct((chunk_rows + NORM_ROWS, LANES), jnp.bfloat16)
    (mark,) = call(
        mark_kernel, "mark", (slab,), (), [jax.ShapeDtypeStruct((8, LANES), jnp.int32)], 1, flops=4*10**9
    )
    mine, others = call(
        pack_kernel,
        "pack",
        (slab,),
        (
            mark,
            queries,
            passages,
            jnp.concatenate([query_lognorm, passage_lognorm]).reshape(1, -1),
            swapped(queries),
            swapped(passages),
            swapped(query_lognorm).reshape(1, -1),
        ),
        [packed, packed],
        4,
    )

    (loss,) = call(
        spread_kernel,
        "spread",
        (loss_cotangent,),
        (),
        [jax.ShapeDtypeStruct((SIZE_ROWS, LANES), jnp.float32)],
        1,
        flops=10**9,
    )

    a_parts, b_parts = [mine], [others]
    for turn in range(1, count):
        back = [(to, at) for at, to in plan.group_pairs(turn)]
        a_parts.append(lax.ppermute(mine, AXES, back))
        b_parts.append(swapped(a_parts[-1]))

    scalars = (slab, blk)
    turns = list(range(count))
    last = turns[1:3]
    soon = [i for i in turns if i not in last]
    a_others = a_parts[1:]
    other_rows = 2 * rows * (count - 1)
    early = call(
        functools.partial(early_kernel, plan, rows, turns[1:], soon),
        "early",
        scalars,
        (loss, *a_others, *(b_parts[i] for i in soon)),
        [
            jax.ShapeDtypeStruct((other_rows, width), jnp.float32),
            jax.ShapeDtypeStruct((other_rows, LANES), jnp.float32),
        ],
        3 * count,
        flops=10**9,
    )
    partials = call(
        functools.partial(late_kernel, plan, rows, turns[1:], last),
        "late",
        scalars,
        (*early, *a_others, *(b_parts[i] for i in last)),
        [
            jax.ShapeDtypeStruct((chunk_rows // 2 + n * SIZE_ROWS, LANES), jnp.float32)
            for n in (3, 5)
        ]
        + [jax.ShapeDtypeStruct((chunk_rows + SIZE_ROWS, LANES), jnp.float32)] * (count - 2),
        3 * count,
    )
    (own,) = call(
        functools.partial(own_kernel, plan, rows, turns),
        "own",
        scalars,
        (mine, *b_parts),
        [jax.ShapeDtypeStruct((2 * rows, width), jnp.float32)],
        3 * count,
        flops=10**9,
    )
    half = jax.ShapeDtypeStruct((rows, width), jnp.float32)

    def crossed(partial, turn, across=False):
        return lax.ppermute(partial.astype(jnp.float16), AXES, plan.group_pairs(turn, across))

    def wide(block):
        return block.astype(jnp.float32)

    arrived = [crossed(x, turn) for turn, x in enumerate(partials[2:], 2)]
    last = [wide(crossed(partials[0], 1)), wide(crossed(partials[1], 1, True))]
    piece = jax.ShapeDtypeStruct((chunk_rows // 2 + 2 * SIZE_ROWS, LANES), jnp.float32)
    keep, give = call(
        sum_kernel, "sum", (), (own, *(wide(x) for x in arrived[:-1])), [half, piece], 2 * count
    )
    got = wide(swapped(give.astype(jnp.float16)))
    there = wide(swapped(arrived[-1][chunk_rows // 2 :]))
    return call(
        end_kernel,
        "end",
        (slab,),
        (loss, keep, wide(arrived[-1]), got, there, *last),
        [half, half],
        4,
    )


def solution(mesh):
    plan = Plan(mesh.shape["slab"], mesh.shape["blk"])
    return jax.shard_map(
        functools.partial(local, plan),
        mesh=mesh,
        in_specs=(
            P(("slab", "blk"), None),
            P(("blk", "slab"), None),
            P(("slab", "blk")),
            P("blk"),
            P(),
        ),
        out_specs=(P(("slab", "blk"), None), P(("blk", "slab"), None)),
        check_vma=False,
    )
```
